512 devices in a mesh: cluster: 32 (over z, x), member: 16 (over y, core).
Axes of the slice: x: 4, y: 8, z: 8, core: 2. Of those that a mesh axis runs over, the one named last changes fastest.
Arguments:
- dual_ops: bfloat16 [32, 16, 1024, 1024], P('cluster', 'member')
- dual_rhs: float32 [32, 16, 1024, 128], P('cluster', 'member'), may hold values from -6 to 6
- rigid_modes: float32 [32, 16, 6, 1024], P('cluster', 'member'), may hold values from -6 to 6
- coarse_rows: float32 [32, 16, 6, 3072], P('cluster', 'member')
- start_coeffs: float32 [32, 16, 6, 128], P('cluster', 'member'), may hold values from -4 to 4
- face_counts: int32 [32, 16, 4], P('cluster', 'member'), may hold values from 0 to 64, as said below
Outputs:
- multipliers: float32 [32, 16, 1024, 128], P('cluster', 'member')
- projected: float32 [32, 16, 1024, 128], P('cluster', 'member')
The draws below stay inside these ranges and needn't reach their ends.
Inputs may be any that keep to these rules, and one draw needn't show every extreme that they name: `face_counts`: equal on both sides of a face, zero on faces at the slab's edges; some face holds exactly 64.
All inputs are finite; a program needn't handle non-finite values.
Results may differ from the reference program's by a relative error of at most 0.0027.
Values sent between devices are 32-bit elements; how exact they have to be, the bound alone decides.
A program may use at most 64 MiB of HBM per device.

```python
import math
import jax
import jax.numpy as jnp
from jax import lax

M = 1024
CAP = 64
R = 128
ITERS = 2
NXS = 32
NYS = 16
NC = 3072


def draw_dual_ops(key, part):
    key = jax.random.fold_in(key, 11)

    def single(index):
        subkey = jax.random.fold_in(key, index)
        first_key, second_key = jax.random.split(subkey)
        base = jax.random.uniform(first_key, (M, M), jnp.float32, -1.0, 1.0)
        coupling = (base + base.T) * (0.8 / math.sqrt(M))
        diagonal = jnp.exp(jax.random.uniform(second_key, (M,), jnp.float32, math.log(2.0), math.log(4.0)))
        on_diagonal = jnp.arange(M)[:, None] == jnp.arange(M)[None, :]
        return jnp.where(on_diagonal, diagonal[:, None], coupling).astype(jnp.bfloat16)
    stacked = lax.map(single, jnp.arange(NXS * NYS, dtype=jnp.int32))
    return stacked.reshape(NXS, NYS, M, M)


def draw_coarse_rows(key, part):
    key = jax.random.fold_in(key, 23)
    shape = (NXS, NYS, 6, NC)
    noise = jax.random.normal(key, shape, jnp.float32)
    owner = (jnp.arange(NXS)[:, None, None, None] * NYS + jnp.arange(NYS)[None, :, None, None]) * 6 + jnp.arange(6)[None, None, :, None]
    on_diagonal = owner == jnp.arange(NC)[None, None, None, :]
    return (jnp.where(on_diagonal, 1.5, 0.0) + noise * (0.5 / math.sqrt(NC))) / M


def draw_face_counts(key, part):
    key = jax.random.fold_in(key, 37)
    first_key, second_key = jax.random.split(key)
    x_pairs = jax.random.randint(first_key, (NXS - 1, NYS), CAP // 2, CAP + 1).astype(jnp.int32)
    x_pairs = x_pairs.at[0, 0].set(CAP)
    y_pairs = jax.random.randint(second_key, (NXS, NYS - 1), CAP // 2, CAP + 1).astype(jnp.int32)
    zero_x = jnp.zeros((1, NYS), jnp.int32)
    zero_y = jnp.zeros((NXS, 1), jnp.int32)
    west = jnp.concatenate([zero_x, x_pairs], 0)
    east = jnp.concatenate([x_pairs, zero_x], 0)
    south = jnp.concatenate([zero_y, y_pairs], 1)
    north = jnp.concatenate([y_pairs, zero_y], 1)
    return jnp.stack([west, east, south, north], 2)


def block_scale(key, dims, cuts, low, high):
    def one(axis_at, shards_of):
        steps = jax.random.uniform(jax.random.fold_in(jax.random.fold_in(key, 6), axis_at), (shards_of,), jnp.float32, low / len(cuts), high / len(cuts))
        return jnp.repeat(jnp.exp(steps), dims[axis_at] // shards_of).reshape((-1,) + (1,) * (len(dims) - axis_at - 1))

    gain = one(*cuts[0])
    for cut in cuts[1:]:
        gain = gain * one(*cut)
    return gain


def centred(own_key, dims, scale, limit, pieces=(), kind=jnp.bfloat16):
    factor_of = block_scale(own_key, dims, pieces, -0.22, 0.18) if pieces else 1.0
    values = jax.random.normal(own_key, dims, jnp.float32) * scale * factor_of
    return jnp.minimum(jnp.maximum(values, -limit), limit).astype(kind)


def setup_inputs(seed: int = 0) -> dict:
    splits = jax.random.split(jax.random.key(seed), 7)
    return {
        "dual_ops": draw_dual_ops(jax.random.fold_in(splits[6], 71), 0),
        "dual_rhs": centred(splits[1], (NXS, NYS, M, R), 1.0, 6.0, ((0, 32), (1, 16)), jnp.float32),
        "rigid_modes": centred(splits[2], (NXS, NYS, 6, M), 1.0, 6.0, ((0, 32), (1, 16)), jnp.float32),
        "coarse_rows": draw_coarse_rows(jax.random.fold_in(splits[6], 71), 0),
        "start_coeffs": centred(splits[4], (NXS, NYS, 6, R), 0.3, 4.0, ((0, 32), (1, 16)), jnp.float32),
        "face_counts": draw_face_counts(jax.random.fold_in(splits[6], 71), 0),
    }


HIGH = lax.Precision.HIGHEST


def starts_of(counts):
    first = counts[0] * 0
    return [first, counts[0], counts[0] + counts[1], counts[0] + counts[1] + counts[2]]


def face_blocks(field, counts):
    starts = starts_of(counts)
    row_ids = jnp.arange(CAP, dtype=jnp.int32)
    blocks = []
    for face in range(4):
        part_rows = lax.dynamic_slice_in_dim(field, starts[face].astype(jnp.int32), CAP, 0)
        blocks.append(jnp.where((row_ids < counts[face])[:, None], part_rows, jnp.zeros_like(part_rows)))
    return jnp.stack(blocks)


def subtract_faces(field, counts, received):
    starts = starts_of(counts)
    row_ids = jnp.arange(CAP, dtype=jnp.int32)
    for face in range(4):
        start = starts[face].astype(jnp.int32)
        part_rows = lax.dynamic_slice_in_dim(field, start, CAP, 0)
        taken = jnp.where((row_ids < counts[face])[:, None], received[face], jnp.zeros_like(part_rows))
        field = lax.dynamic_update_slice_in_dim(field, part_rows - taken, start, 0)
    return field


def assemble(field, face_counts):
    blocks = jax.vmap(jax.vmap(face_blocks))(field, face_counts)
    zero_x = jnp.zeros_like(blocks[:1, :, 0])
    from_west = jnp.concatenate([zero_x, blocks[:-1, :, 1]], 0)
    from_east = jnp.concatenate([blocks[1:, :, 0], zero_x], 0)
    zero_y = jnp.zeros_like(blocks[:, :1, 0])
    from_south = jnp.concatenate([zero_y, blocks[:, :-1, 3]], 1)
    from_north = jnp.concatenate([blocks[:, 1:, 2], zero_y], 1)
    received = jnp.stack([from_west, from_east, from_south, from_north], 2)
    return jax.vmap(jax.vmap(subtract_faces))(field, face_counts, received)


def reference(dual_ops, dual_rhs, rigid_modes, coarse_rows, start_coeffs, face_counts):
    faces_total = jnp.sum(face_counts, axis=2)
    slot_ids = jnp.arange(M, dtype=jnp.int32)
    weights = jnp.where(slot_ids[None, None, :] < faces_total[:, :, None], 0.5, 1.0).astype(jnp.float32)[..., None]
    flat_ops = dual_ops.reshape(NXS * NYS, M, M)
    inverse = coarse_rows.reshape(NC, NC)

    def inner_product(left, right):
        return jnp.sum(weights * left * right, axis=(0, 1, 2))

    def apply_dual(field):
        rounded = field.astype(jnp.bfloat16).reshape(NXS * NYS, M, R)
        result = lax.map(lambda pair: jnp.dot(pair[0], pair[1], preferred_element_type=jnp.float32), (flat_ops, rounded))
        return result.reshape(NXS, NYS, M, R)

    def expand_modes(coeffs):
        return jnp.einsum("xykm,xykr->xymr", rigid_modes, coeffs, precision=HIGH)

    def coarse_coeffs(field):
        products = jnp.einsum("xykm,xymr->xykr", rigid_modes, field, precision=HIGH).reshape(NC, R)
        return jnp.dot(inverse, products, precision=HIGH, preferred_element_type=jnp.float32).reshape(NXS, NYS, 6, R)

    multipliers = assemble(expand_modes(start_coeffs), face_counts)
    residual = assemble(dual_rhs - apply_dual(multipliers), face_counts)
    projected = residual - assemble(expand_modes(coarse_coeffs(residual)), face_counts)
    direction = projected
    norm_now = inner_product(projected, projected)
    for iteration in range(ITERS):
        image = assemble(apply_dual(direction), face_counts)
        alpha = norm_now / inner_product(direction, image)
        multipliers = multipliers + alpha * direction
        residual = residual - alpha * image
        projected = residual - assemble(expand_modes(coarse_coeffs(residual)), face_counts)
        norm_next = inner_product(projected, projected)
        direction = projected + (norm_next / norm_now) * direction
        norm_now = norm_next
    return multipliers, projected
```

```python
import functools

import jax
import jax.numpy as jnp
from jax import lax
from jax.experimental import pallas as pl
from jax.experimental.pallas import tpu as pltpu
from jax.sharding import PartitionSpec as P

CAP = 64
TOP = 4 * CAP
MESH = pl.DeviceIdType.MESH
F32 = jnp.float32
BF16 = jnp.bfloat16


def dot(a, b):
    return jnp.dot(a, b, preferred_element_type=F32)


def split(x):
    high = x.astype(BF16)
    return high, (x - high.astype(F32)).astype(BF16)


def far_first(t, n):
    return n // 2 + ((t % 2) * 2 - 1) * ((t + 1) // 2)


def kernel(
    ncl, nme, nx,
    ops_hbm, rhs_hbm, modes_hbm, rows_hbm, start_hbm, counts,
    m_ref, p_ref,
    ops, rhs, modes, rows, start,
    b32, bb, bt, pad, hs, hb,
    v_ref, r_ref, p0_ref, u0_ref, p1_ref, im_ref,
    s1_send, s1_buf, q_send, q_buf, f_send, f_buf,
    g_buf, t_buf, t_send, c_buf, g3_buf, t3_buf, t3_send,
    local_sem, s1_sems, h_sems, q_sems, f_sems, g_sems, t_sems, c_sems,
):
    i, j = lax.axis_index("cluster"), lax.axis_index("member")
    nz = ncl // nx
    west, east = (lax.rem(i + ncl - 1, ncl), j), (lax.rem(i + 1, ncl), j)
    south, north = (i, lax.rem(j + nme - 1, nme)), (i, lax.rem(j + 1, nme))
    sides = (west, east, south, north)

    def member_peer(t):
        return lax.rem(j + far_first(t, nme), nme)

    def cluster_peer(t):
        z = lax.rem(i // nx + far_first(t // nx, nz), nz)
        x = lax.rem(i % nx + far_first(t % nx, nx), nx)
        return z * nx + x

    def over_members(body):
        lax.fori_loop(0, nme - 1, lambda t, _: (body(member_peer(t)), 0)[1], 0)

    def over_cluster(body):
        lax.fori_loop(0, ncl - 1, lambda t, _: (body(cluster_peer(t)), 0)[1], 0)

    def send(src, dst, sems, device):
        pltpu.make_async_remote_copy(
            src, dst, sems.at[0], sems.at[1], device_id=device, device_id_type=MESH
        ).start()

    def wait(ref, sem):
        pltpu.make_async_copy(ref, ref, sem).wait()

    barrier = pltpu.get_barrier_semaphore()

    def greet(device):
        pl.semaphore_signal(barrier, inc=1, device_id=device, device_id_type=MESH)

    over_cluster(lambda peer: greet((peer, j)))
    over_members(lambda peer: greet((i, peer)))

    loads = [
        pltpu.make_async_copy(src, dst, local_sem.at[n])
        for n, (src, dst) in enumerate(
            ((modes_hbm, modes), (start_hbm, start), (rows_hbm, rows), (ops_hbm, ops), (rhs_hbm, rhs))
        )
    ]
    for load in loads:
        load.start()

    first = [counts[0] * 0, counts[0], counts[0] + counts[1], counts[0] + counts[1] + counts[2]]
    in_faces = first[3] + counts[3]
    face_rows = lax.broadcasted_iota(jnp.int32, (CAP, 128), 0)

    def face_of(ref, f):
        block = ref[pl.ds(first[f], CAP), :]
        return jnp.where(face_rows < counts[f], block, 0.0)

    pad[...] = jnp.zeros_like(pad)

    loads[0].wait()
    loads[1].wait()
    slots = modes.shape[1]
    v_ref[...] = jnp.concatenate([modes[...], jnp.zeros((122, slots), F32)], 0).T
    start8 = jnp.concatenate([start[...], jnp.zeros((2, 128), F32)], 0)
    for f in range(4):
        s1_send[f, 0:CAP, :] = face_of(v_ref, f)
        s1_send[f, CAP : CAP + 8, :] = start8

    loads[2].wait()
    wide, cols = 8 * nme, 6 * nme
    spread = (
        lax.broadcasted_iota(jnp.int32, (cols, wide), 1)
        == (lax.broadcasted_iota(jnp.int32, (cols, wide), 0) // 6) * 8
        + lax.broadcasted_iota(jnp.int32, (cols, wide), 0) % 6
    ).astype(BF16)
    stacked = jnp.concatenate(
        [
            jnp.concatenate([rows[:, k * cols : (k + 1) * cols], jnp.zeros((2, cols), F32)], 0)
            for k in range(ncl)
        ],
        0,
    )
    high, low = split(stacked)
    placed = dot(high, spread) + dot(low, spread)
    row8 = lax.broadcasted_iota(jnp.int32, (8 * ncl, wide), 0) % 8
    col8 = lax.broadcasted_iota(jnp.int32, (8 * ncl, wide), 1) % 8
    placed = placed + jnp.where((row8 == col8) & (row8 >= 6), 1.0, 0.0)
    hs[...] = placed.reshape(ncl, 8, wide)
    hb[i] = hs[i]

    pl.semaphore_wait(barrier, ncl + nme - 2)

    for f in range(4):
        send(s1_send.at[f], s1_buf.at[f ^ 1], s1_sems, sides[f])
    over_cluster(lambda peer: send(hs.at[peer], hb.at[i], h_sems, (peer, j)))

    b32[...] = v_ref[...]
    wait(s1_buf, s1_sems.at[1])
    top = b32[0:TOP, :]
    for f in range(4):
        pad[f, TOP : TOP + CAP, :] = s1_buf[f, 0:CAP, :]
    for f in range(4):
        top = top - pltpu.roll(pad[f, pl.ds(TOP - first[f], TOP), :], 8 * (f + 1), 1)
    b32[0:TOP, :] = top
    lane = lax.broadcasted_iota(jnp.int32, (slots, 128), 1)
    b_high, b_low = split(b32[...])
    b_high, b_low = b_high.astype(F32), b_low.astype(F32)
    packed = jnp.where(
        lane < 40, b_high, jnp.where(lane < 80, pltpu.roll(b_high, 40, 1), pltpu.roll(b_low, 80, 1))
    )
    bb[...] = packed.astype(BF16)
    bt[...] = packed.T.astype(BF16)

    def expand(coeffs):
        high, low = split(coeffs)
        return dot(bb[...], jnp.concatenate([high, low, high, jnp.zeros((8, 128), BF16)], 0))

    def products(field):
        high, low = split(field)
        both = dot(bt[...], high)
        return both[0:40] + both[80:120] + dot(bt[0:40, :], low)

    def assemble(ref, k):
        wait(f_buf.at[k], f_sems.at[k, 1])
        for f in range(4):
            pad[f, TOP : TOP + CAP, :] = f_buf[k, f]
        top = ref[0:TOP, :]
        for f in range(4):
            top = top - pad[f, pl.ds(TOP - first[f], TOP), :]
        ref[0:TOP, :] = top

    def send_faces(ref, k):
        for f in range(4):
            f_send[k, f] = face_of(ref, f)
            send(f_send.at[k, f], f_buf.at[k, f ^ 1], f_sems.at[k], sides[f])

    tile_row = lax.broadcasted_iota(jnp.int32, (8, 128), 0)

    def inner_rows(product):
        return jnp.sum(product, 0, keepdims=True)

    def weighted(field):
        top_rows = lax.broadcasted_iota(jnp.int32, (TOP, 128), 0)
        square = field * field
        return inner_rows(square) - 0.5 * inner_rows(
            jnp.where(top_rows < in_faces, square[0:TOP], 0.0)
        )

    def gather_modes(field, k):
        terms = products(field)
        q_send[k] = terms[8:40].reshape(4, 8, 128)
        for f in range(4):
            send(q_send.at[k, f], q_buf.at[k, f ^ 1], q_sems.at[k], sides[f])
        return terms[0:8]

    def coarse(k, own, scalars):
        wait(q_buf.at[k], q_sems.at[k, 1])
        tile = own + q_buf[k, 0] + q_buf[k, 1] + q_buf[k, 2] + q_buf[k, 3]
        for n, scalar in enumerate(scalars[:2]):
            tile = jnp.where(tile_row == 6 + n, scalar, tile)
        h_high, h_low = split(hb[...].reshape(8 * ncl, wide))
        third = len(scalars) == 3
        gathered = g3_buf if third else g_buf.at[k]
        sending = t3_send if third else t_send.at[k]
        summing = t3_buf if third else t_buf.at[k]
        if third:
            gathered[j, 0:8, :] = tile
            gathered[j, 8:9, :] = scalars[2]
        else:
            gathered[j] = tile
        over_members(lambda peer: send(gathered.at[j], gathered.at[j], g_sems.at[k], (i, peer)))
        wait(gathered.at[0 : nme - 1], g_sems.at[k, 1])
        g_high, g_low = split(gathered[:, 0:8, :].reshape(wide, 128))
        part = dot(h_high, g_high) + dot(h_high, g_low) + dot(h_low, g_high)
        sending[:, 0:8, :] = part.reshape(ncl, 8, 128)
        if third:
            last = jnp.sum(gathered[:, 8:9, :], 0, keepdims=True)
            sending[:, 8:9, :] = jnp.broadcast_to(last, (ncl, 1, 128))
        summing[i] = sending[i]
        over_cluster(lambda peer: send(sending.at[peer], summing.at[i], t_sems.at[k], (peer, j)))
        wait(summing.at[0 : ncl - 1], t_sems.at[k, 1])
        total = jnp.sum(summing[:, 0:8, :], 0)
        c_buf[k, 0] = jnp.where(tile_row < 6, total, 0.0)
        for f in range(4):
            send(c_buf.at[k, 0], c_buf.at[k, 1 + (f ^ 1)], c_sems.at[k], sides[f])
        sums = [total[6:7], total[7:8]]
        if third:
            sums.append(jnp.sum(summing[:, 8:9, :], 0))
        return sums

    def coefficients(k):
        wait(c_buf.at[k, 1:5], c_sems.at[k, 1])
        return c_buf[k].reshape(40, 128)

    starts = jnp.concatenate([start8] + [s1_buf[f, CAP : CAP + 8, :] for f in range(4)], 0)
    m_ref[...] = expand(starts)
    loads[3].wait()
    loads[4].wait()
    r_ref[...] = rhs[...] - dot(ops[...], m_ref[...].astype(BF16))
    own = gather_modes(r_ref[...], 0)
    send_faces(r_ref, 0)
    wait(hb.at[0 : ncl - 1], h_sems.at[1])
    coarse(0, own, [])
    assemble(r_ref, 0)
    coeffs0 = coefficients(0)
    p0_ref[...] = r_ref[...] - expand(coeffs0)

    u0_ref[...] = dot(ops[...], p0_ref[...].astype(BF16))
    own = gather_modes(u0_ref[...], 1)
    send_faces(u0_ref, 1)
    norm0, curv0 = coarse(
        1, own, [weighted(p0_ref[...]), inner_rows(p0_ref[...] * u0_ref[...])]
    )
    im_ref[...] = u0_ref[...]
    assemble(im_ref, 1)
    alpha0 = norm0 / curv0
    r_ref[...] = r_ref[...] - alpha0 * im_ref[...]
    image_coeffs = coefficients(1)
    coeffs1 = coeffs0 - alpha0 * image_coeffs
    p1_ref[...] = r_ref[...] - expand(coeffs1)

    high, low = split(p1_ref[...])
    v_ref[...] = dot(ops[...], high) + dot(ops[...], low)
    own = gather_modes(v_ref[...], 2)
    send_faces(v_ref, 2)
    norm1, curv1, cross = coarse(
        2,
        own,
        [
            weighted(p1_ref[...]),
            inner_rows(p1_ref[...] * v_ref[...]),
            inner_rows(p1_ref[...] * u0_ref[...] + p0_ref[...] * v_ref[...]),
        ],
    )
    beta = norm1 / norm0
    alpha1 = norm1 / (curv1 + beta * (cross + beta * curv0))
    assemble(v_ref, 2)
    m_ref[...] = m_ref[...] + (alpha0 + alpha1 * beta) * p0_ref[...] + alpha1 * p1_ref[...]
    r_ref[...] = r_ref[...] - alpha1 * (v_ref[...] + beta * im_ref[...])
    coeffs2 = coeffs1 - alpha1 * (coefficients(2) + beta * image_coeffs)
    p_ref[...] = r_ref[...] - expand(coeffs2)

    wait(s1_buf, s1_sems.at[0])
    wait(hb.at[0 : ncl - 1], h_sems.at[0])
    for k in range(3):
        wait(q_buf.at[k], q_sems.at[k, 0])
        wait(f_buf.at[k], f_sems.at[k, 0])
        gathered, summing = (g3_buf, t3_buf) if k == 2 else (g_buf.at[k], t_buf.at[k])
        wait(gathered.at[0 : nme - 1], g_sems.at[k, 0])
        wait(summing.at[0 : ncl - 1], t_sems.at[k, 0])
        wait(c_buf.at[k, 1:5], c_sems.at[k, 0])


def solution(mesh):
    ncl, nme = mesh.shape["cluster"], mesh.shape["member"]
    nx = 4 if ncl % 4 == 0 else 1

    def per_device(dual_ops, dual_rhs, rigid_modes, coarse_rows, start_coeffs, face_counts):
        slots, cases = dual_rhs.shape[2:]
        field = pltpu.VMEM((slots, cases), F32)
        out = jax.ShapeDtypeStruct((slots, cases), F32)
        multipliers, projected = pl.pallas_call(
            functools.partial(kernel, ncl, nme, nx),
            out_shape=(out, out),
            in_specs=[pl.BlockSpec(memory_space=pl.ANY)] * 5
            + [pl.BlockSpec(memory_space=pltpu.SMEM)],
            out_specs=(pl.BlockSpec(memory_space=pltpu.VMEM),) * 2,
            scratch_shapes=[
                pltpu.VMEM((slots, slots), BF16),
                field,
                pltpu.VMEM((6, slots), F32),
                pltpu.VMEM((6, 6 * ncl * nme), F32),
                pltpu.VMEM((6, cases), F32),
                field,
                pltpu.VMEM((slots, 128), BF16),
                pltpu.VMEM((128, slots), BF16),
                pltpu.VMEM((4, 2 * TOP + CAP, cases), F32),
                pltpu.VMEM((ncl, 8, 8 * nme), F32),
                pltpu.VMEM((ncl, 8, 8 * nme), F32),
                field, field, field, field, field, field,
                pltpu.VMEM((4, CAP + 8, cases), F32),
                pltpu.VMEM((4, CAP + 8, cases), F32),
                pltpu.VMEM((3, 4, 8, cases), F32),
                pltpu.VMEM((3, 4, 8, cases), F32),
                pltpu.VMEM((3, 4, CAP, cases), F32),
                pltpu.VMEM((3, 4, CAP, cases), F32),
                pltpu.VMEM((2, nme, 8, cases), F32),
                pltpu.VMEM((2, ncl, 8, cases), F32),
                pltpu.VMEM((2, ncl, 8, cases), F32),
                pltpu.VMEM((3, 5, 8, cases), F32),
                pltpu.VMEM((nme, 9, cases), F32),
                pltpu.VMEM((ncl, 9, cases), F32),
                pltpu.VMEM((ncl, 9, cases), F32),
                pltpu.SemaphoreType.DMA((5,)),
                pltpu.SemaphoreType.DMA((2,)),
                pltpu.SemaphoreType.DMA((2,)),
                pltpu.SemaphoreType.DMA((3, 2)),
                pltpu.SemaphoreType.DMA((3, 2)),
                pltpu.SemaphoreType.DMA((3, 2)),
                pltpu.SemaphoreType.DMA((3, 2)),
                pltpu.SemaphoreType.DMA((3, 2)),
            ],
            compiler_params=pltpu.CompilerParams(
                collective_id=0, has_side_effects=True, vmem_limit_bytes=48 << 20
            ),
            name="cg",
        )(
            dual_ops[0, 0], dual_rhs[0, 0], rigid_modes[0, 0], coarse_rows[0, 0],
            start_coeffs[0, 0], face_counts[0, 0],
        )
        return multipliers[None, None], projected[None, None]

    whole = P("cluster", "member", None, None)
    return jax.shard_map(
        per_device,
        mesh=mesh,
        in_specs=(whole,) * 5 + (P("cluster", "member", None),),
        out_specs=(whole, whole),
        check_vma=False,
    )
```

```python
import functools

import jax
import jax.numpy as jnp
from jax import lax
from jax.experimental import pallas as pl
from jax.experimental.pallas import tpu as pltpu
from jax.sharding import PartitionSpec as P

CAP = 64
TOP = 4 * CAP
MESH = pl.DeviceIdType.MESH
F32 = jnp.float32
BF16 = jnp.bfloat16

STEPS = (
    (0, 0), (-1, 0), (1, 0), (0, -1), (0, 1),
    (-2, 0), (2, 0), (0, -2), (0, 2), (-1, -1), (-1, 1), (1, -1), (1, 1),
)


def slot_of(one, two=(0, 0)):
    return STEPS.index((one[0] + two[0], one[1] + two[1]))


def opposite(slot):
    return STEPS.index((-STEPS[slot][0], -STEPS[slot][1]))


def dot(a, b):
    return jnp.dot(a, b, preferred_element_type=F32)


def split(x):
    high = x.astype(BF16)
    return high, (x - high.astype(F32)).astype(BF16)


def far_first(t, n):
    return n // 2 + ((t % 2) * 2 - 1) * ((t + 1) // 2)


def kernel(
    ncl, nme, nx,
    ops_hbm, rhs_hbm, modes_hbm, rows_hbm, start_hbm, counts,
    m_ref, p_ref,
    ops, rhs, modes, rows, start,
    bb, bt, ft, pad, hs, hb, h2, k13,
    v_ref, r_ref, p0_ref, u0_ref, p1_ref, im_ref,
    s1_send, s1_buf, q_send, q_buf, f_send, f_buf,
    g_buf, t_buf, t_send, c_buf, sg_buf, st_buf, st_send,
    local_sem, s1_sems, h_sems, q_sems, f_sems, g_sems, t_sems, c_sems, sg_sems, st_sems,
):
    i, j = lax.axis_index("cluster"), lax.axis_index("member")
    nz = ncl // nx
    wide, cols = 8 * nme, 6 * nme
    slots = ops.shape[0]

    def at_step(slot):
        di, dj = STEPS[slot]
        return lax.rem(i + (di + ncl), ncl), lax.rem(j + (dj + nme), nme)

    def member_peer(t):
        return lax.rem(j + far_first(t, nme), nme)

    def cluster_peer(t):
        z = lax.rem(i // nx + far_first(t // nx, nz), nz)
        x = lax.rem(i % nx + far_first(t % nx, nx), nx)
        return z * nx + x

    def over_members(body):
        lax.fori_loop(0, nme - 1, lambda t, _: (body(member_peer(t)), 0)[1], 0, unroll=UNROLL)

    def over_cluster(body):
        lax.fori_loop(0, ncl - 1, lambda t, _: (body(cluster_peer(t)), 0)[1], 0, unroll=UNROLL)

    def send(src, dst, sems, device):
        pltpu.make_async_remote_copy(
            src, dst, sems.at[0], sems.at[1], device_id=device, device_id_type=MESH
        ).start()

    def wait(ref, sem):
        pltpu.make_async_copy(ref, ref, sem).wait()

    loads = [
        pltpu.make_async_copy(src, dst, local_sem.at[n])
        for n, (src, dst) in enumerate(
            ((modes_hbm, modes), (start_hbm, start), (rows_hbm, rows), (ops_hbm, ops), (rhs_hbm, rhs))
        )
    ]
    for load in loads:
        load.start()

    barrier = pltpu.get_barrier_semaphore()

    def greet(device):
        pl.semaphore_signal(barrier, inc=1, device_id=device, device_id_type=MESH)

    for slot in range(9, 13):
        greet(at_step(slot))
    over_cluster(lambda peer: greet((peer, j)))
    over_members(lambda peer: greet((i, peer)))

    first = [counts[0] * 0, counts[0], counts[0] + counts[1], counts[0] + counts[1] + counts[2]]
    in_faces = first[3] + counts[3]
    face_rows = lax.broadcasted_iota(jnp.int32, (CAP, 128), 0)
    tile_row = lax.broadcasted_iota(jnp.int32, (8, 128), 0)
    tile_lane = lax.broadcasted_iota(jnp.int32, (8, 128), 1)

    def face_of(ref, f):
        block = ref[pl.ds(first[f], CAP), :]
        return jnp.where(face_rows < counts[f], block, 0.0)

    loads[0].wait()
    loads[1].wait()
    modes8 = jnp.concatenate([modes[:, 0, :], jnp.zeros((2, slots), F32)], 0)
    start8 = jnp.concatenate([start[:, 0, :], jnp.zeros((2, 128), F32)], 0)
    for f in range(4):
        turned = pltpu.roll(modes8[:, 0:TOP], lax.rem(TOP - first[f], TOP), 1)[:, 0:128]
        s1_send[f, 0:8, :] = jnp.where(tile_lane < counts[f], turned, 0.0)
        s1_send[f, 8:16, :] = start8

    pl.semaphore_wait(barrier, ncl + nme + 2)
    for f in range(4):
        send(s1_send.at[f], s1_buf.at[f ^ 1], s1_sems, at_step(f + 1))

    loads[2].wait()
    spread = (
        lax.broadcasted_iota(jnp.int32, (cols, wide), 1)
        == (lax.broadcasted_iota(jnp.int32, (cols, wide), 0) // 6) * 8
        + lax.broadcasted_iota(jnp.int32, (cols, wide), 0) % 6
    ).astype(BF16)
    row_values = jnp.concatenate([rows[:, 0, :], jnp.zeros((2, cols * ncl), F32)], 0)
    high, low = split(
        jnp.concatenate([row_values[:, k * cols : (k + 1) * cols] for k in range(ncl)], 0)
    )
    hs[...] = (dot(high, spread) + dot(low, spread)).reshape(ncl, 8, wide)
    hb[i] = hs[i]
    over_cluster(lambda peer: send(hs.at[peer], hb.at[i], h_sems, (peer, j)))

    pad[...] = jnp.zeros_like(pad)
    g_buf[:, :, 6:8, :] = jnp.zeros((3, nme, 2, 128), F32)
    c_buf[:, :, 6:8, :] = jnp.zeros((3, 13, 2, 128), F32)

    def pack(lo, hi, across):
        high, low = split(across)
        high, low = high.astype(F32), low.astype(F32)
        none = jnp.zeros((8, hi - lo), F32)
        bt[0:48, lo:hi] = jnp.concatenate([high, none], 0).astype(BF16)
        bt[48:96, lo:hi] = jnp.concatenate([low, none], 0).astype(BF16)
        bb[lo:hi, :] = jnp.concatenate([high, high, low, none], 0).T.astype(BF16)

    def expand(coeffs, lo=0, hi=None):
        high, low = split(coeffs)
        return dot(bb[lo:hi, :], jnp.concatenate([high, low, high, jnp.zeros((8, 128), BF16)], 0))

    pack(TOP, slots, jnp.concatenate([modes8[:, TOP:], jnp.zeros((32, slots - TOP), F32)], 0))
    m_ref[TOP:, :] = expand(jnp.concatenate([start8, jnp.zeros((32, 128), F32)], 0), TOP)
    loads[3].wait()
    loads[4].wait()
    r_ref[...] = rhs[...] - dot(ops[:, TOP:], m_ref[TOP:, :].astype(BF16))

    wait(s1_buf, s1_sems.at[1])
    across = [modes8[:, 0:TOP]]
    for f in range(4):
        block = jnp.concatenate([s1_buf[f, 0:8, :], jnp.zeros((8, TOP - 128), F32)], 1)
        across.append(-pltpu.roll(block, first[f], 1))
    pack(0, TOP, jnp.concatenate(across, 0))

    def times(parts, field):
        high, low = split(field)
        both = dot(parts[...], high)
        return both[0:40] + both[48:88] + dot(parts[0:48, :], low)[0:40]

    def assemble(ref, k):
        wait(f_buf.at[k], f_sems.at[k, 1])
        for f in range(4):
            pad[f, TOP : TOP + CAP, :] = f_buf[k, f]
        top = ref[0:TOP, :]
        for f in range(4):
            top = top - pad[f, pl.ds(TOP - first[f], TOP), :]
        ref[0:TOP, :] = top

    def send_faces(ref, k):
        for f in range(4):
            f_send[k, f] = face_of(ref, f)
            send(f_send.at[k, f], f_buf.at[k, f ^ 1], f_sems.at[k], at_step(f + 1))

    def send_terms(terms, k):
        q_send[k] = terms[8:40].reshape(4, 8, 128)
        for f in range(4):
            send(q_send.at[k, f], q_buf.at[k, f ^ 1], q_sems.at[k], at_step(f + 1))
        return terms[0:8]

    def received_terms(k):
        wait(q_buf.at[k], q_sems.at[k, 1])
        return q_buf[k, 0] + q_buf[k, 1] + q_buf[k, 2] + q_buf[k, 3]

    def inner_rows(product):
        return jnp.sum(product, 0, keepdims=True)

    def weighted(field):
        top_rows = lax.broadcasted_iota(jnp.int32, (TOP, 128), 0)
        square = field * field
        return inner_rows(square) - 0.5 * inner_rows(
            jnp.where(top_rows < in_faces, square[0:TOP], 0.0)
        )

    def gather(k, tile):
        mine = g_buf.at[k, j, pl.ds(0, 6)]
        g_buf[k, j] = tile
        over_members(lambda peer: send(mine, mine, g_sems.at[k], (i, peer)))

    def scatter(k):
        wait(g_buf.at[k, 0 : nme - 1, pl.ds(0, 6)], g_sems.at[k, 1])
        g_high, g_low = split(g_buf[k].reshape(wide, 128))
        part = dot(h2[...], jnp.concatenate([g_high, g_high], 0)) + dot(h2[:, 0:wide], g_low)
        t_send[k] = part.reshape(ncl, 8, 128)
        t_buf[k, i] = t_send[k, i]
        over_cluster(
            lambda peer: send(
                t_send.at[k, peer, pl.ds(0, 6)], t_buf.at[k, i, pl.ds(0, 6)], t_sems.at[k], (peer, j)
            )
        )

    def share(k, around):
        wait(t_buf.at[k, 0 : ncl - 1, pl.ds(0, 6)], t_sems.at[k, 1])
        total = jnp.sum(t_buf[k], 0)
        c_buf[k, 0] = jnp.where(tile_row < 6, total, 0.0)
        mine = c_buf.at[k, 0, pl.ds(0, 6)]
        for slot in range(around - 1, 0, -1):
            send(mine, c_buf.at[k, opposite(slot), pl.ds(0, 6)], c_sems.at[k], at_step(slot))

    def shared(k, around):
        wait(c_buf.at[k, 1:around, pl.ds(0, 6)], c_sems.at[k, 1])

    def near(k):
        return c_buf[k, 0:5].reshape(40, 128)

    def coupled(k):
        high, low = split(c_buf[k].reshape(104, 128))
        fill = jnp.zeros((24, 128), BF16)
        high, low = jnp.concatenate([high, fill], 0), jnp.concatenate([low, fill], 0)
        both = dot(k13[...], high)
        return both[0:8] + both[8:16] + dot(k13[...], low)[0:8]

    def gather_sums(k, sums):
        sg_buf[k, j] = jnp.concatenate(sums, 0)
        mine = sg_buf.at[k, j]
        over_members(lambda peer: send(mine, mine, sg_sems.at[k], (i, peer)))

    def scatter_sums(k):
        wait(sg_buf.at[k, 0 : nme - 1], sg_sems.at[k, 1])
        total = jnp.sum(sg_buf[k], 0)
        st_send[k] = total
        st_buf[k, i] = total
        over_cluster(lambda peer: send(st_send.at[k], st_buf.at[k, i], st_sems.at[k], (peer, j)))

    def sums(k):
        wait(st_buf.at[k, 0 : ncl - 1], st_sems.at[k, 1])
        total = jnp.sum(st_buf[k], 0)
        return total[0:1], total[1:2], total[2:3]

    starts = jnp.concatenate([start8] + [s1_buf[f, 8:16, :] for f in range(4)], 0)
    m_ref[0:TOP, :] = expand(starts, 0, TOP)
    r_ref[...] = r_ref[...] - dot(ops[:, 0:TOP], m_ref[0:TOP, :].astype(BF16))
    own = send_terms(times(bt, r_ref[...]), 0)

    gather(0, own + received_terms(0))
    send_faces(r_ref, 0)

    both = dot(bt[...], ops[...])
    high, low = split(both[0:48] + both[48:96])
    ft[0:48, :] = high
    ft[48:96, :] = low
    both = dot(ft[...], bb[...])
    own_rows = send_terms(both[0:40] + both[48:88] + pltpu.roll(both[0:40], 48, 1), 1)
    assemble(r_ref, 0)
    gr_own = send_terms(times(ft, r_ref[...]), 2)
    wait(hb.at[0 : ncl - 1], h_sems.at[1])
    high, low = split(hb[...].reshape(8 * ncl, wide))
    h2[:, 0:wide] = high
    h2[:, wide : 2 * wide] = low
    scatter(0)
    wait(q_buf.at[1], q_sems.at[1, 1])
    around_rows = jnp.where(tile_lane < 40, own_rows, 0.0)
    for f in range(4):
        for n in range(5):
            slot = slot_of(STEPS[f + 1], STEPS[n])
            moved = q_buf[1, f]
            if slot != n:
                moved = pltpu.roll(moved, (8 * (slot - n)) % 128, 1)
            around_rows = around_rows + jnp.where(
                (tile_lane >= 8 * slot) & (tile_lane < 8 * slot + 8), moved, 0.0
            )
    high, low = split(around_rows)
    k13[...] = jnp.concatenate([high, low], 0)
    gr = gr_own + received_terms(2)
    share(0, 13)
    shared(0, 13)
    tile1 = gr - coupled(0)
    gather(1, tile1)

    p0_ref[...] = r_ref[...] - expand(near(0))
    u0_ref[...] = dot(ops[...], p0_ref[...].astype(BF16))
    send_faces(u0_ref, 1)
    gather_sums(
        0,
        [weighted(p0_ref[...]), inner_rows(p0_ref[...] * u0_ref[...]), jnp.zeros((1, 128), F32)],
    )
    scatter(1)
    im_ref[...] = u0_ref[...]
    assemble(im_ref, 1)
    gi_own = send_terms(times(ft, im_ref[...]), 3)
    scatter_sums(0)
    gi = gi_own + received_terms(3)
    share(1, 13)
    norm0, curv0, _ = sums(0)
    alpha0 = norm0 / curv0
    r_ref[...] = r_ref[...] - alpha0 * im_ref[...]
    shared(1, 13)
    gather(2, tile1 - alpha0 * (gi - coupled(1)))

    coeffs1 = near(0) - alpha0 * near(1)
    p1_ref[...] = r_ref[...] - expand(coeffs1)
    high, low = split(p1_ref[...])
    v_ref[...] = dot(ops[...], high) + dot(ops[...], low)
    send_faces(v_ref, 2)
    gather_sums(
        1,
        [
            weighted(p1_ref[...]),
            inner_rows(p1_ref[...] * v_ref[...]),
            inner_rows(p1_ref[...] * u0_ref[...] + p0_ref[...] * v_ref[...]),
        ],
    )
    scatter(2)
    scatter_sums(1)
    assemble(v_ref, 2)
    share(2, 5)
    norm1, curv1, cross = sums(1)
    beta = norm1 / norm0
    alpha1 = norm1 / (curv1 + beta * (cross + beta * curv0))
    m_ref[...] = m_ref[...] + (alpha0 + alpha1 * beta) * p0_ref[...] + alpha1 * p1_ref[...]
    r_ref[...] = r_ref[...] - alpha1 * (v_ref[...] + beta * im_ref[...])
    shared(2, 5)
    p_ref[...] = r_ref[...] - expand(coeffs1 - alpha1 * (near(2) + beta * near(1)))

    wait(s1_buf, s1_sems.at[0])
    wait(hb.at[0 : ncl - 1], h_sems.at[0])
    for k in range(4):
        wait(q_buf.at[k], q_sems.at[k, 0])
    for k in range(3):
        wait(f_buf.at[k], f_sems.at[k, 0])
        wait(g_buf.at[k, 0 : nme - 1, pl.ds(0, 6)], g_sems.at[k, 0])
        wait(t_buf.at[k, 0 : ncl - 1, pl.ds(0, 6)], t_sems.at[k, 0])
        wait(c_buf.at[k, 1 : (13, 13, 5)[k], pl.ds(0, 6)], c_sems.at[k, 0])
    for k in range(2):
        wait(sg_buf.at[k, 0 : nme - 1], sg_sems.at[k, 0])
        wait(st_buf.at[k, 0 : ncl - 1], st_sems.at[k, 0])


UNROLL = True
PIECES = 4


def finish(m_in, p_in, m_out, p_out, held, sems):
    size = m_in.shape[0] // PIECES
    pairs = [
        (src.at[pl.ds(n * size, size)], held.at[k, n], dst.at[pl.ds(n * size, size)], sems.at[0, k, n], sems.at[1, k, n])
        for k, (src, dst) in enumerate(((m_in, m_out), (p_in, p_out)))
        for n in range(PIECES)
    ]
    for src, here, _, sem, _ in pairs:
        pltpu.make_async_copy(src, here, sem).start()
    for src, here, dst, sem, sem2 in pairs:
        pltpu.make_async_copy(src, here, sem).wait()
        pltpu.make_async_copy(here, dst, sem2).start()
    for _, here, dst, _, sem2 in pairs:
        pltpu.make_async_copy(here, dst, sem2).wait()


def solution(mesh):
    ncl, nme = mesh.shape["cluster"], mesh.shape["member"]
    nx = 4 if ncl % 4 == 0 else 1

    def per_device(dual_ops, dual_rhs, rigid_modes, coarse_rows, start_coeffs, face_counts):
        slots, cases = dual_rhs.shape[2:]
        field = pltpu.VMEM((slots, cases), F32)
        out = jax.ShapeDtypeStruct((slots, cases), F32)

        def by_row(x):
            return x.reshape(x.shape[2], 1, x.shape[3])

        multipliers, projected = pl.pallas_call(
            functools.partial(kernel, ncl, nme, nx),
            out_shape=(out, out),
            in_specs=[pl.BlockSpec(memory_space=pltpu.HBM)] * 5
            + [pl.BlockSpec(memory_space=pltpu.SMEM)],
            out_specs=(pl.BlockSpec(memory_space=pltpu.VMEM),) * 2,
            scratch_shapes=[
                pltpu.VMEM((slots, slots), BF16),
                field,
                pltpu.VMEM((6, 1, slots), F32),
                pltpu.VMEM((6, 1, 6 * ncl * nme), F32),
                pltpu.VMEM((6, 1, cases), F32),
                pltpu.VMEM((slots, 128), BF16),
                pltpu.VMEM((96, slots), BF16),
                pltpu.VMEM((96, slots), BF16),
                pltpu.VMEM((4, 2 * TOP + CAP, cases), F32),
                pltpu.VMEM((ncl, 8, 8 * nme), F32),
                pltpu.VMEM((ncl, 8, 8 * nme), F32),
                pltpu.VMEM((8 * ncl, 16 * nme), BF16),
                pltpu.VMEM((16, 128), BF16),
                field, field, field, field, field, field,
                pltpu.VMEM((4, 16, cases), F32),
                pltpu.VMEM((4, 16, cases), F32),
                pltpu.VMEM((4, 4, 8, cases), F32),
                pltpu.VMEM((4, 4, 8, cases), F32),
                pltpu.VMEM((3, 4, CAP, cases), F32),
                pltpu.VMEM((3, 4, CAP, cases), F32),
                pltpu.VMEM((3, nme, 8, cases), F32),
                pltpu.VMEM((3, ncl, 8, cases), F32),
                pltpu.VMEM((3, ncl, 8, cases), F32),
                pltpu.VMEM((3, 13, 8, cases), F32),
                pltpu.VMEM((2, nme, 3, cases), F32),
                pltpu.VMEM((2, ncl, 3, cases), F32),
                pltpu.VMEM((2, 3, cases), F32),
                pltpu.SemaphoreType.DMA((5,)),
                pltpu.SemaphoreType.DMA((2,)),
                pltpu.SemaphoreType.DMA((2,)),
                pltpu.SemaphoreType.DMA((4, 2)),
                pltpu.SemaphoreType.DMA((3, 2)),
                pltpu.SemaphoreType.DMA((3, 2)),
                pltpu.SemaphoreType.DMA((3, 2)),
                pltpu.SemaphoreType.DMA((3, 2)),
                pltpu.SemaphoreType.DMA((2, 2)),
                pltpu.SemaphoreType.DMA((2, 2)),
            ],
            compiler_params=pltpu.CompilerParams(
                collective_id=0, has_side_effects=True, vmem_limit_bytes=60 << 20
            ),
            name="cg",
        )(
            dual_ops[0, 0], dual_rhs[0, 0], by_row(rigid_modes), by_row(coarse_rows),
            by_row(start_coeffs), face_counts[0, 0],
        )
        multipliers, projected = pl.pallas_call(
            finish,
            out_shape=(out, out),
            in_specs=[pl.BlockSpec(memory_space=pl.ANY)] * 2,
            out_specs=(pl.BlockSpec(memory_space=pl.ANY),) * 2,
            scratch_shapes=[pltpu.VMEM((2, PIECES, slots // PIECES, cases), F32), pltpu.SemaphoreType.DMA((2, 2, PIECES))],
            name="finish",
        )(multipliers, projected)
        return multipliers[None, None], projected[None, None]

    whole = P("cluster", "member", None, None)
    return jax.shard_map(
        per_device,
        mesh=mesh,
        in_specs=(whole,) * 5 + (P("cluster", "member", None),),
        out_specs=(whole, whole),
        check_vma=False,
    )
```

```python
import functools

import jax
import jax.numpy as jnp
from jax import lax
from jax.experimental import pallas as pl
from jax.experimental.pallas import tpu as pltpu
from jax.sharding import PartitionSpec as P

CAP = 64
TOP = 4 * CAP
MESH = pl.DeviceIdType.MESH
F32 = jnp.float32
BF16 = jnp.bfloat16

STEPS = (
    (0, 0), (-1, 0), (1, 0), (0, -1), (0, 1),
)


def opposite(slot):
    return STEPS.index((-STEPS[slot][0], -STEPS[slot][1]))


def dot(a, b):
    return jnp.dot(a, b, preferred_element_type=F32)


def split(x):
    high = x.astype(BF16)
    return high, (x - high.astype(F32)).astype(BF16)


def far_first(t, n):
    return n // 2 + ((t % 2) * 2 - 1) * ((t + 1) // 2)


def kernel(
    ncl, nme, nx,
    ops_hbm, rhs_hbm, modes_hbm, rows_hbm, start_hbm, counts,
    m_hbm, p_hbm,
    m_ref, p_ref, ops, rhs, modes, rows, start,
    bb, bt, ft, pad, hs, hb, h2, m2, h_near, a_high, a_low, d_high, d_low, v_send, v_buf,
    v_ref, r_ref, p0_ref, u0_ref, q_ref, im_ref,
    s1_send, s1_buf, q_send, q_buf, f_send, f_buf,
    g_buf, e_buf, x_buf, t_buf, t_send, c_buf, sg_buf, st_buf, st_send,
    local_sem, s1_sems, h_sems, q_sems, f_sems, g_sems, e_sems, x_sems, near_sems, v_sems,
    t_sems, c_sems, sg_sems, st_sems,
):
    i, j = lax.axis_index("cluster"), lax.axis_index("member")
    nz = ncl // nx
    wide, cols = 8 * nme, 6 * nme
    slots = ops.shape[0]

    def at_step(slot):
        di, dj = STEPS[slot]
        return lax.rem(i + (di + ncl), ncl), lax.rem(j + (dj + nme), nme)

    def member_peer(t):
        return lax.rem(j + far_first(t, nme), nme)

    def cluster_peer(t):
        z = lax.rem(i // nx + far_first(t // nx, nz), nz)
        x = lax.rem(i % nx + far_first(t % nx, nx), nx)
        return z * nx + x

    def over_members(body):
        lax.fori_loop(0, nme - 1, lambda t, _: (body(member_peer(t)), 0)[1], 0, unroll=UNROLL)

    def over_cluster(body):
        lax.fori_loop(0, ncl - 1, lambda t, _: (body(cluster_peer(t)), 0)[1], 0, unroll=UNROLL)

    def send(src, dst, sems, device):
        pltpu.make_async_remote_copy(
            src, dst, sems.at[0], sems.at[1], device_id=device, device_id_type=MESH
        ).start()

    def store(n, src, dst, lo, hi):
        return pltpu.make_async_copy(src.at[lo:hi], dst.at[lo:hi], local_sem.at[5 + n])

    def wait(ref, sem):
        pltpu.make_async_copy(ref, ref, sem).wait()

    loads = [
        pltpu.make_async_copy(src, dst, local_sem.at[n])
        for n, (src, dst) in enumerate(
            ((modes_hbm, modes), (start_hbm, start), (rows_hbm, rows), (ops_hbm, ops), (rhs_hbm, rhs))
        )
    ]
    for load in loads:
        load.start()

    barrier = pltpu.get_barrier_semaphore()

    def greet(device):
        pl.semaphore_signal(barrier, inc=1, device_id=device, device_id_type=MESH)

    over_cluster(lambda peer: greet((peer, j)))
    over_members(lambda peer: greet((i, peer)))

    first = [counts[0] * 0, counts[0], counts[0] + counts[1], counts[0] + counts[1] + counts[2]]
    in_faces = first[3] + counts[3]
    face_rows = lax.broadcasted_iota(jnp.int32, (CAP, 128), 0)
    tile_row = lax.broadcasted_iota(jnp.int32, (8, 128), 0)
    tile_lane = lax.broadcasted_iota(jnp.int32, (8, 128), 1)

    def face_of(ref, f):
        block = ref[pl.ds(first[f], CAP), :]
        return jnp.where(face_rows < counts[f], block, 0.0)

    loads[0].wait()
    loads[1].wait()
    modes8 = jnp.concatenate([modes[:, 0, :], jnp.zeros((2, slots), F32)], 0)
    start8 = jnp.concatenate([start[:, 0, :], jnp.zeros((2, 128), F32)], 0)
    for f in range(4):
        turned = pltpu.roll(modes8[:, 0:TOP], lax.rem(TOP - first[f], TOP), 1)[:, 0:128]
        s1_send[f, 0:8, :] = jnp.where(tile_lane < counts[f], turned, 0.0)
        s1_send[f, 8:16, :] = start8

    pl.semaphore_wait(barrier, ncl + nme - 2)
    for f in range(4):
        send(s1_send.at[f], s1_buf.at[f ^ 1], s1_sems, at_step(f + 1))

    loads[2].wait()
    spread = (
        lax.broadcasted_iota(jnp.int32, (cols, wide), 1)
        == (lax.broadcasted_iota(jnp.int32, (cols, wide), 0) // 6) * 8
        + lax.broadcasted_iota(jnp.int32, (cols, wide), 0) % 6
    ).astype(BF16)
    row_values = jnp.concatenate([rows[:, 0, :], jnp.zeros((2, cols * ncl), F32)], 0)
    high, low = split(
        jnp.concatenate([row_values[:, k * cols : (k + 1) * cols] for k in range(ncl)], 0)
    )
    hs[...] = (dot(high, spread) + dot(low, spread)).reshape(ncl, 8, wide)
    hb[i] = hs[i]
    over_cluster(lambda peer: send(hs.at[peer], hb.at[i], h_sems, (peer, j)))

    pad[...] = jnp.zeros_like(pad)
    g_buf[:, :, 6:8, :] = jnp.zeros((3, nme, 2, 128), F32)
    e_buf[:, :, 6:8, :] = jnp.zeros((2, nme, 2, 128), F32)
    c_buf[:, :, 6:8, :] = jnp.zeros((3, 5, 2, 128), F32)

    def pack(lo, hi, across):
        high, low = split(across)
        high, low = high.astype(F32), low.astype(F32)
        none = jnp.zeros((8, hi - lo), F32)
        bt[0:48, lo:hi] = jnp.concatenate([high, none], 0).astype(BF16)
        bt[48:96, lo:hi] = jnp.concatenate([low, none], 0).astype(BF16)
        bb[lo:hi, :] = jnp.concatenate([high, high, low, none], 0).T.astype(BF16)

    def expand(coeffs, lo=0, hi=None):
        high, low = split(coeffs)
        return dot(bb[lo:hi, :], jnp.concatenate([high, low, high, jnp.zeros((8, 128), BF16)], 0))

    pack(TOP, slots, jnp.concatenate([modes8[:, TOP:], jnp.zeros((32, slots - TOP), F32)], 0))
    m_ref[TOP:, :] = expand(jnp.concatenate([start8, jnp.zeros((32, 128), F32)], 0), TOP)
    loads[3].wait()
    loads[4].wait()
    r_ref[...] = rhs[...] - dot(ops[:, TOP:], m_ref[TOP:, :].astype(BF16))

    wait(s1_buf, s1_sems.at[1])
    across = [modes8[:, 0:TOP]]
    for f in range(4):
        block = jnp.concatenate([s1_buf[f, 0:8, :], jnp.zeros((8, TOP - 128), F32)], 1)
        across.append(-pltpu.roll(block, first[f], 1))
    pack(0, TOP, jnp.concatenate(across, 0))

    def times(parts, field):
        high, low = split(field)
        both = dot(parts[...], high)
        return both[0:40] + both[48:88] + dot(parts[0:48, :], low)[0:40]

    def assemble(ref, k):
        wait(f_buf.at[k], f_sems.at[k, 1])
        for f in range(4):
            pad[f, TOP : TOP + CAP, :] = f_buf[k, f]
        top = ref[0:TOP, :]
        for f in range(4):
            top = top - pad[f, pl.ds(TOP - first[f], TOP), :]
        ref[0:TOP, :] = top

    def send_faces(ref, k):
        for f in range(4):
            f_send[k, f] = face_of(ref, f)
            send(f_send.at[k, f], f_buf.at[k, f ^ 1], f_sems.at[k], at_step(f + 1))

    def send_terms(terms, k):
        q_send[k] = terms[8:40].reshape(4, 8, 128)
        for f in range(4):
            send(q_send.at[k, f], q_buf.at[k, f ^ 1], q_sems.at[k], at_step(f + 1))
        return terms[0:8]

    def received_terms(k):
        wait(q_buf.at[k], q_sems.at[k, 1])
        return q_buf[k, 0] + q_buf[k, 1] + q_buf[k, 2] + q_buf[k, 3]

    def inner_rows(product):
        return jnp.sum(product, 0, keepdims=True)

    def weighted(field):
        top_rows = lax.broadcasted_iota(jnp.int32, (TOP, 128), 0)
        square = field * field
        return inner_rows(square) - 0.5 * inner_rows(
            jnp.where(top_rows < in_faces, square[0:TOP], 0.0)
        )

    def gather(buf, sems, k, tile):
        mine = buf.at[k, j, pl.ds(0, 6)]
        buf[k, j] = tile
        over_members(lambda peer: send(mine, mine, sems.at[k], (i, peer)))

    def gathered(buf, sems, k):
        wait(buf.at[k, 0 : nme - 1, pl.ds(0, 6)], sems.at[k, 1])
        return split(buf[k].reshape(wide, 128))

    def two_part(matrix, parts):
        high, low = parts
        return dot(matrix[...], jnp.concatenate([high, high], 0)) + dot(matrix[:, 0:wide], low)

    def scatter(k):
        if k == 0:
            part = two_part(h2, gathered(g_buf, g_sems, 0))
        else:
            base = two_part(h2, gathered(e_buf, e_sems, k - 1))
            part = base - two_part(m2, gathered(g_buf, g_sems, k))
        t_send[k] = part.reshape(ncl, 8, 128)
        t_buf[k, i] = t_send[k, i]
        over_cluster(
            lambda peer: send(
                t_send.at[k, peer, pl.ds(0, 6)], t_buf.at[k, i, pl.ds(0, 6)], t_sems.at[k], (peer, j)
            )
        )

    def share(k):
        wait(t_buf.at[k, 0 : ncl - 1, pl.ds(0, 6)], t_sems.at[k, 1])
        tile = jnp.where(tile_row < 6, jnp.sum(t_buf[k], 0), 0.0)
        c_buf[k, 0] = tile
        mine = c_buf.at[k, 0, pl.ds(0, 6)]
        for slot in range(1, 5):
            send(mine, c_buf.at[k, opposite(slot), pl.ds(0, 6)], c_sems.at[k], at_step(slot))
        if k < 2:
            gather(g_buf, g_sems, k + 1, tile)

    def alone(k):
        return jnp.concatenate([c_buf[k, 0], jnp.zeros((32, 128), F32)], 0)

    def near(k):
        wait(c_buf.at[k, 1:5, pl.ds(0, 6)], c_sems.at[k, 1])
        return c_buf[k].reshape(40, 128)

    def apply(out, field, columns):
        both = dot(ops[:, columns], jnp.concatenate(split(field[columns, :]), 1))
        return out + both[:, 0:128] + both[:, 128:256]

    upper, lower = slice(0, TOP), slice(TOP, slots)

    starts = jnp.concatenate([start8] + [s1_buf[f, 8:16, :] for f in range(4)], 0)
    m_ref[0:TOP, :] = expand(starts, 0, TOP)
    r_ref[...] = r_ref[...] - dot(ops[:, 0:TOP], m_ref[0:TOP, :].astype(BF16))
    own = send_terms(times(bt, r_ref[...]), 0)

    gather(g_buf, g_sems, 0, own + received_terms(0))
    send_faces(r_ref, 0)

    both = dot(bt[...], ops[...])
    high, low = split(both[0:48] + both[48:96])
    ft[0:48, :] = high
    ft[48:96, :] = low
    both = dot(ft[...], bb[...])
    x = both[0:40] + both[48:88] + pltpu.roll(both[0:40], 48, 1)
    x = jnp.where(lax.broadcasted_iota(jnp.int32, (40, 128), 1) < 40, x, 0.0)
    mine = x_buf.at[j]
    x_buf[j] = (
        x[0:16]
        + pltpu.roll(x[16:32], 40, 1)
        + pltpu.roll(jnp.concatenate([x[32:40], jnp.zeros((8, 128), F32)], 0), 80, 1)
    )
    over_members(lambda peer: send(mine, mine, x_sems, (i, peer)))

    wait(hb.at[0 : ncl - 1], h_sems.at[1])
    high, low = split(hb[...].reshape(8 * ncl, wide))
    h2[:, 0:wide] = high
    h2[:, wide : 2 * wide] = low
    assemble(r_ref, 0)
    gr_own = send_terms(times(ft, r_ref[...]), 1)
    scatter(0)
    for n, step in enumerate((2, 1)):
        send(hb.at[:, pl.ds(0, 6)], h_near.at[n, :, pl.ds(0, 6)], near_sems.at[n], at_step(step))
    gather(e_buf, e_sems, 0, gr_own + received_terms(1))

    wait(x_buf.at[0 : nme - 1], x_sems.at[1])
    lanes = 5 * wide
    q_row = lax.broadcasted_iota(jnp.int32, (128, lanes), 0)
    q_lane = lax.broadcasted_iota(jnp.int32, (128, lanes), 1)
    source = (q_lane // wide) * 8 + q_lane % 8
    for n in range(5):
        q = (q_row == source + 40 * (n // 2)).astype(BF16)
        half = 8 * (n % 2)
        high, low = split(x_buf[:, half : half + 8, :].reshape(wide, 128))
        d_row = lax.broadcasted_iota(jnp.int32, (wide, lanes), 0)
        d_lane = lax.broadcasted_iota(jnp.int32, (wide, lanes), 1)
        same = d_row // 8 == (d_lane % wide) // 8
        d_high[n * wide : (n + 1) * wide, :] = jnp.where(same, dot(high, q), 0.0).astype(BF16)
        d_low[n * wide : (n + 1) * wide, :] = jnp.where(same, dot(low, q), 0.0).astype(BF16)
    share(0)
    for n in range(2):
        wait(h_near.at[n, :, pl.ds(0, 6)], near_sems.at[n, 1])
    mid = hb[...].reshape(8 * ncl, wide)
    groups = [mid] + [h_near[n].reshape(8 * ncl, wide) for n in range(2)]
    groups += [pltpu.roll(mid, 8, 1), pltpu.roll(mid, wide - 8, 1)]
    for n, group in enumerate(groups):
        high, low = split(group)
        a_high[:, n * wide : (n + 1) * wide] = high
        a_low[:, n * wide : (n + 1) * wide] = low

    def group_of(n):
        at = slice(n * wide, (n + 1) * wide)
        return (
            dot(a_high[...], d_high[:, at]) + dot(a_high[...], d_low[:, at]) + dot(a_low[...], d_high[:, at])
        )

    for n in range(2):
        v_send[n] = group_of(n + 1).reshape(ncl, 8, wide)
        send(
            v_send.at[n, :, pl.ds(0, 6)], v_buf.at[n, :, pl.ds(0, 6)], v_sems.at[n], at_step(n + 1)
        )
    v_ref[0 : 8 * ncl, 0:wide] = (
        group_of(0) + pltpu.roll(group_of(3), wide - 8, 1) + pltpu.roll(group_of(4), 8, 1)
    )

    p0_ref[lower, :] = r_ref[lower, :] - expand(alone(0), TOP)
    u0_ref[...] = apply(0.0, p0_ref, lower)
    p0_ref[upper, :] = r_ref[upper, :] - expand(near(0), 0, TOP)
    u0_ref[...] = apply(u0_ref[...], p0_ref, upper)
    send_faces(u0_ref, 1)
    for n in range(2):
        wait(v_buf.at[n, :, pl.ds(0, 6)], v_sems.at[n, 1])
    high, low = split(
        v_ref[0 : 8 * ncl, 0:wide]
        + v_buf[0].reshape(8 * ncl, wide)
        + v_buf[1].reshape(8 * ncl, wide)
    )
    m2[:, 0:wide] = high
    m2[:, wide : 2 * wide] = low
    scatter(1)
    im_ref[...] = u0_ref[...]
    assemble(im_ref, 1)
    gi_own = send_terms(times(ft, im_ref[...]), 2)
    sum_rows = [weighted(p0_ref[...]), inner_rows(p0_ref[...] * u0_ref[...])]
    gather(e_buf, e_sems, 1, gi_own + received_terms(2))
    share(1)

    q_ref[lower, :] = im_ref[lower, :] - expand(alone(1), TOP)
    v_ref[...] = apply(0.0, q_ref, lower)
    q_ref[upper, :] = im_ref[upper, :] - expand(near(1), 0, TOP)
    v_ref[...] = apply(v_ref[...], q_ref, upper)
    sum_rows += [
        weighted(q_ref[...]),
        inner_rows(q_ref[...] * v_ref[...]),
        inner_rows(p0_ref[...] * v_ref[...] + q_ref[...] * u0_ref[...]),
    ]
    in_face = lax.broadcasted_iota(jnp.int32, (TOP, 128), 0) < in_faces
    cross = p0_ref[...] * q_ref[...]
    sum_rows.append(inner_rows(cross) - 0.5 * inner_rows(jnp.where(in_face, cross[upper], 0.0)))
    sg_buf[j] = jnp.concatenate(sum_rows, 0)
    mine = sg_buf.at[j]
    over_members(lambda peer: send(mine, mine, sg_sems, (i, peer)))
    send_faces(v_ref, 2)
    scatter(2)
    wait(sg_buf.at[0 : nme - 1], sg_sems.at[1])
    st_send[...] = jnp.sum(sg_buf[...], 0)
    st_buf[i] = st_send[...]
    over_cluster(lambda peer: send(st_send, st_buf.at[i], st_sems, (peer, j)))
    assemble(v_ref, 2)
    share(2)
    v_ref[lower, :] = v_ref[lower, :] - expand(alone(2), TOP)
    wait(st_buf.at[0 : ncl - 1], st_sems.at[1])
    total = jnp.sum(st_buf[...], 0)
    norm0, curv0, norm_q, curv_q, curv_pq, norm_pq = [total[n : n + 1] for n in range(6)]
    alpha0 = norm0 / curv0
    norm1 = norm0 - alpha0 * (2.0 * norm_pq - alpha0 * norm_q)
    beta = norm1 / norm0
    scale = 1.0 + beta
    alpha1 = norm1 / (scale * (scale * curv0 - alpha0 * curv_pq) + alpha0 * alpha0 * curv_q)
    first_by = alpha0 + alpha1 * scale
    second_by = alpha0 * alpha1
    m_ref[...] = m_ref[...] + first_by * p0_ref[...] - second_by * q_ref[...]
    store(0, m_ref, m_hbm, 0, slots).start()
    p_ref[lower, :] = p0_ref[lower, :] - first_by * q_ref[lower, :] + second_by * v_ref[lower, :]
    store(1, p_ref, p_hbm, TOP, slots).start()
    last = p0_ref[upper, :] - first_by * q_ref[upper, :] + second_by * v_ref[upper, :]
    p_ref[upper, :] = last - second_by * expand(near(2), 0, TOP)
    store(2, p_ref, p_hbm, 0, TOP).start()

    store(0, m_ref, m_hbm, 0, slots).wait()
    store(1, p_ref, p_hbm, TOP, slots).wait()
    store(2, p_ref, p_hbm, 0, TOP).wait()
    wait(s1_buf, s1_sems.at[0])
    wait(hb.at[0 : ncl - 1], h_sems.at[0])
    wait(x_buf.at[0 : nme - 1], x_sems.at[0])
    for n in range(2):
        wait(h_near.at[n, :, pl.ds(0, 6)], near_sems.at[n, 0])
        wait(v_buf.at[n, :, pl.ds(0, 6)], v_sems.at[n, 0])
        wait(e_buf.at[n, 0 : nme - 1, pl.ds(0, 6)], e_sems.at[n, 0])
    for k in range(3):
        wait(q_buf.at[k], q_sems.at[k, 0])
        wait(f_buf.at[k], f_sems.at[k, 0])
        wait(g_buf.at[k, 0 : nme - 1, pl.ds(0, 6)], g_sems.at[k, 0])
        wait(t_buf.at[k, 0 : ncl - 1, pl.ds(0, 6)], t_sems.at[k, 0])
        wait(c_buf.at[k, 1:5, pl.ds(0, 6)], c_sems.at[k, 0])
    wait(sg_buf.at[0 : nme - 1], sg_sems.at[0])
    wait(st_buf.at[0 : ncl - 1], st_sems.at[0])


UNROLL = True
PIECES = 4


def finish(m_in, p_in, m_out, p_out, held, sems):
    size = m_in.shape[0] // PIECES
    pairs = [
        (src.at[pl.ds(n * size, size)], held.at[k, n], dst.at[pl.ds(n * size, size)], sems.at[0, k, n], sems.at[1, k, n])
        for k, (src, dst) in enumerate(((m_in, m_out), (p_in, p_out)))
        for n in range(PIECES)
    ]
    for src, here, _, sem, _ in pairs:
        pltpu.make_async_copy(src, here, sem).start()
    for src, here, dst, sem, sem2 in pairs:
        pltpu.make_async_copy(src, here, sem).wait()
        pltpu.make_async_copy(here, dst, sem2).start()
    for _, here, dst, _, sem2 in pairs:
        pltpu.make_async_copy(here, dst, sem2).wait()


def solution(mesh):
    ncl, nme = mesh.shape["cluster"], mesh.shape["member"]
    nx = 4 if ncl % 4 == 0 else 1

    def per_device(dual_ops, dual_rhs, rigid_modes, coarse_rows, start_coeffs, face_counts):
        slots, cases = dual_rhs.shape[2:]
        field = pltpu.VMEM((slots, cases), F32)
        out = jax.ShapeDtypeStruct((slots, cases), F32)

        def by_row(x):
            return x.reshape(x.shape[2], 1, x.shape[3])

        multipliers, projected = pl.pallas_call(
            functools.partial(kernel, ncl, nme, nx),
            out_shape=(out, out),
            in_specs=[pl.BlockSpec(memory_space=pltpu.HBM)] * 5
            + [pl.BlockSpec(memory_space=pltpu.SMEM)],
            out_specs=(pl.BlockSpec(memory_space=pl.ANY),) * 2,
            scratch_shapes=[
                field, field,
                pltpu.VMEM((slots, slots), BF16),
                field,
                pltpu.VMEM((6, 1, slots), F32),
                pltpu.VMEM((6, 1, 6 * ncl * nme), F32),
                pltpu.VMEM((6, 1, cases), F32),
                pltpu.VMEM((slots, 128), BF16),
                pltpu.VMEM((96, slots), BF16),
                pltpu.VMEM((96, slots), BF16),
                pltpu.VMEM((4, 2 * TOP + CAP, cases), F32),
                pltpu.VMEM((ncl, 8, 8 * nme), F32),
                pltpu.VMEM((ncl, 8, 8 * nme), F32),
                pltpu.VMEM((8 * ncl, 16 * nme), BF16),
                pltpu.VMEM((8 * ncl, 16 * nme), BF16),
                pltpu.VMEM((2, ncl, 8, 8 * nme), F32),
                pltpu.VMEM((8 * ncl, 40 * nme), BF16),
                pltpu.VMEM((8 * ncl, 40 * nme), BF16),
                pltpu.VMEM((40 * nme, 40 * nme), BF16),
                pltpu.VMEM((40 * nme, 40 * nme), BF16),
                pltpu.VMEM((2, ncl, 8, 8 * nme), F32),
                pltpu.VMEM((2, ncl, 8, 8 * nme), F32),
                field, field, field, field, field, field,
                pltpu.VMEM((4, 16, cases), F32),
                pltpu.VMEM((4, 16, cases), F32),
                pltpu.VMEM((3, 4, 8, cases), F32),
                pltpu.VMEM((3, 4, 8, cases), F32),
                pltpu.VMEM((3, 4, CAP, cases), F32),
                pltpu.VMEM((3, 4, CAP, cases), F32),
                pltpu.VMEM((3, nme, 8, cases), F32),
                pltpu.VMEM((2, nme, 8, cases), F32),
                pltpu.VMEM((nme, 16, 128), F32),
                pltpu.VMEM((3, ncl, 8, cases), F32),
                pltpu.VMEM((3, ncl, 8, cases), F32),
                pltpu.VMEM((3, 5, 8, cases), F32),
                pltpu.VMEM((nme, 6, cases), F32),
                pltpu.VMEM((ncl, 6, cases), F32),
                pltpu.VMEM((6, cases), F32),
                pltpu.SemaphoreType.DMA((8,)),
                pltpu.SemaphoreType.DMA((2,)),
                pltpu.SemaphoreType.DMA((2,)),
                pltpu.SemaphoreType.DMA((3, 2)),
                pltpu.SemaphoreType.DMA((3, 2)),
                pltpu.SemaphoreType.DMA((3, 2)),
                pltpu.SemaphoreType.DMA((2, 2)),
                pltpu.SemaphoreType.DMA((2,)),
                pltpu.SemaphoreType.DMA((2, 2)),
                pltpu.SemaphoreType.DMA((2, 2)),
                pltpu.SemaphoreType.DMA((3, 2)),
                pltpu.SemaphoreType.DMA((3, 2)),
                pltpu.SemaphoreType.DMA((2,)),
                pltpu.SemaphoreType.DMA((2,)),
            ],
            compiler_params=pltpu.CompilerParams(
                collective_id=0, has_side_effects=True, vmem_limit_bytes=60 << 20
            ),
            name="cg",
        )(
            dual_ops[0, 0], dual_rhs[0, 0], by_row(rigid_modes), by_row(coarse_rows),
            by_row(start_coeffs), face_counts[0, 0],
        )
        multipliers, projected = pl.pallas_call(
            finish,
            out_shape=(out, out),
            in_specs=[pl.BlockSpec(memory_space=pl.ANY)] * 2,
            out_specs=(pl.BlockSpec(memory_space=pl.ANY),) * 2,
            scratch_shapes=[pltpu.VMEM((2, PIECES, slots // PIECES, cases), F32), pltpu.SemaphoreType.DMA((2, 2, PIECES))],
            name="finish",
        )(multipliers, projected)
        return multipliers[None, None], projected[None, None]

    whole = P("cluster", "member", None, None)
    return jax.shard_map(
        per_device,
        mesh=mesh,
        in_specs=(whole,) * 5 + (P("cluster", "member", None),),
        out_specs=(whole, whole),
        check_vma=False,
    )
```

```python
import functools

import jax
import jax.numpy as jnp
from jax import lax
from jax.experimental import pallas as pl
from jax.experimental.pallas import tpu as pltpu
from jax.sharding import PartitionSpec as P

CAP = 64
TOP = 4 * CAP
MESH = pl.DeviceIdType.MESH
F32 = jnp.float32
BF16 = jnp.bfloat16

STEPS = (
    (0, 0), (-1, 0), (1, 0), (0, -1), (0, 1),
)


def opposite(slot):
    return STEPS.index((-STEPS[slot][0], -STEPS[slot][1]))


def dot(a, b):
    return jnp.dot(a, b, preferred_element_type=F32)


def split(x):
    high = x.astype(BF16)
    return high, (x - high.astype(F32)).astype(BF16)


def far_first(t, n):
    return n // 2 + ((t % 2) * 2 - 1) * ((t + 1) // 2)


def kernel(
    ncl, nme, nx,
    ops_hbm, rhs_hbm, modes_hbm, rows_hbm, start_hbm, counts,
    m_hbm, p_hbm,
    m_ref, p_ref, ops, rhs, modes, rows, start,
    bb, bt, ft, pad, hs, hb, h2, m2, h_near, a_high, a_low, d_high, d_low, v_send, v_buf,
    v_ref, r_ref, p0_ref, u0_ref, q_ref, im_ref,
    s1_send, s1_buf, q_send, q_buf, f_send, f_buf,
    g_buf, e_buf, x_buf, t_buf, t_send, c_buf, sg_buf, st_buf, st_send,
    news, local_sem, s1_sems, h_sems, q_sems, f_sems, g_sems, e_sems, x_sems, near_sems, v_sems,
    t_sems, c_sems, sg_sems, st_sems,
):
    i, j = lax.axis_index("cluster"), lax.axis_index("member")
    nz = ncl // nx
    wide, cols = 8 * nme, 6 * nme
    slots = ops.shape[0]

    def at_step(slot):
        di, dj = STEPS[slot]
        return lax.rem(i + (di + ncl), ncl), lax.rem(j + (dj + nme), nme)

    def member_peer(t):
        return lax.rem(j + far_first(t, nme), nme)

    def cluster_peer(t):
        z = lax.rem(i // nx + far_first(t // nx, nz), nz)
        x = lax.rem(i % nx + far_first(t % nx, nx), nx)
        return z * nx + x

    def over_members(body):
        lax.fori_loop(0, nme - 1, lambda t, _: (body(member_peer(t)), 0)[1], 0, unroll=UNROLL)

    def over_cluster(body):
        lax.fori_loop(0, ncl - 1, lambda t, _: (body(cluster_peer(t)), 0)[1], 0, unroll=UNROLL)

    def send(src, dst, sems, device):
        pltpu.make_async_remote_copy(
            src, dst, sems.at[0], sems.at[1], device_id=device, device_id_type=MESH
        ).start()

    def store(n, src, dst, lo, hi):
        return pltpu.make_async_copy(src.at[lo:hi], dst.at[lo:hi], local_sem.at[5 + n])

    def wait(ref, sem):
        pltpu.make_async_copy(ref, ref, sem).wait()

    loads = [
        pltpu.make_async_copy(src, dst, local_sem.at[n])
        for n, (src, dst) in enumerate(
            ((modes_hbm, modes), (start_hbm, start), (rows_hbm, rows), (ops_hbm, ops), (rhs_hbm, rhs))
        )
    ]
    for load in loads:
        load.start()

    barrier = pltpu.get_barrier_semaphore()

    def greet(device):
        pl.semaphore_signal(barrier, inc=1, device_id=device, device_id_type=MESH)

    ny, z, x, y, core = nme // 2, i // nx, i % nx, j // 2, j % 2
    assert nz <= 8 and ny <= 8 and nx in (1, 4)

    def along(axis, step):
        if axis == "z":
            return lax.rem(z + (step + nz), nz) * nx + x, j
        if axis == "x":
            return z * nx + lax.rem(x + (step + nx), nx), j
        return i, lax.rem(y + (step + ny), ny) * 2 + core

    def both_ways(distance, over):
        sizes = (("z", nz), ("y", ny), ("x", nx))
        return [
            along(axis, step) for axis, n in sizes if n > over for step in (-distance, distance)
        ]

    other_core = (i, y * 2 + 1 - core)
    beside = [at_step(slot) for slot in range(1, 5)] + both_ways(1, 1) + [other_core]
    rounds = (
        both_ways(1, 2),
        [along(axis, step) for axis, n in (("z", nz), ("y", ny)) if n > 4 for step in (-2, 2)],
        ([along("x", step) for step in (-1, 1, 2)] if nx > 1 else []) + [other_core],
    )
    for device in beside:
        greet(device)

    def tell(n):
        for device in rounds[n]:
            pl.semaphore_signal(news.at[n], inc=1, device_id=device, device_id_type=MESH)

    def hear(n):
        if rounds[n]:
            pl.semaphore_wait(news.at[n], len(rounds[n]))

    first = [counts[0] * 0, counts[0], counts[0] + counts[1], counts[0] + counts[1] + counts[2]]
    in_faces = first[3] + counts[3]
    face_rows = lax.broadcasted_iota(jnp.int32, (CAP, 128), 0)
    tile_row = lax.broadcasted_iota(jnp.int32, (8, 128), 0)
    tile_lane = lax.broadcasted_iota(jnp.int32, (8, 128), 1)

    def face_of(ref, f):
        block = ref[pl.ds(first[f], CAP), :]
        return jnp.where(face_rows < counts[f], block, 0.0)

    loads[0].wait()
    loads[1].wait()
    modes8 = jnp.concatenate([modes[:, 0, :], jnp.zeros((2, slots), F32)], 0)
    start8 = jnp.concatenate([start[:, 0, :], jnp.zeros((2, 128), F32)], 0)
    for f in range(4):
        turned = pltpu.roll(modes8[:, 0:TOP], lax.rem(TOP - first[f], TOP), 1)[:, 0:128]
        s1_send[f, 0:8, :] = jnp.where(tile_lane < counts[f], turned, 0.0)
        s1_send[f, 8:16, :] = start8

    pl.semaphore_wait(barrier, len(beside))
    for f in range(4):
        send(s1_send.at[f], s1_buf.at[f ^ 1], s1_sems, at_step(f + 1))
    tell(0)

    pad[...] = jnp.zeros_like(pad)
    g_buf[:, :, 6:8, :] = jnp.zeros((3, nme, 2, 128), F32)
    e_buf[:, :, 6:8, :] = jnp.zeros((2, nme, 2, 128), F32)
    c_buf[:, :, 6:8, :] = jnp.zeros((3, 5, 2, 128), F32)

    def pack(lo, hi, across):
        high, low = split(across)
        high, low = high.astype(F32), low.astype(F32)
        none = jnp.zeros((8, hi - lo), F32)
        bt[0:48, lo:hi] = jnp.concatenate([high, none], 0).astype(BF16)
        bt[48:96, lo:hi] = jnp.concatenate([low, none], 0).astype(BF16)
        bb[lo:hi, :] = jnp.concatenate([high, high, low, none], 0).T.astype(BF16)

    def expand(coeffs, lo=0, hi=None):
        high, low = split(coeffs)
        return dot(bb[lo:hi, :], jnp.concatenate([high, low, high, jnp.zeros((8, 128), BF16)], 0))

    hear(0)
    tell(1)

    pack(TOP, slots, jnp.concatenate([modes8[:, TOP:], jnp.zeros((32, slots - TOP), F32)], 0))
    m_ref[TOP:, :] = expand(jnp.concatenate([start8, jnp.zeros((32, 128), F32)], 0), TOP)
    loads[3].wait()
    loads[4].wait()
    r_ref[...] = rhs[...] - dot(ops[:, TOP:], m_ref[TOP:, :].astype(BF16))

    loads[2].wait()
    spread = (
        lax.broadcasted_iota(jnp.int32, (cols, wide), 1)
        == (lax.broadcasted_iota(jnp.int32, (cols, wide), 0) // 6) * 8
        + lax.broadcasted_iota(jnp.int32, (cols, wide), 0) % 6
    ).astype(BF16)
    row_values = jnp.concatenate([rows[:, 0, :], jnp.zeros((2, cols * ncl), F32)], 0)
    high, low = split(
        jnp.concatenate([row_values[:, k * cols : (k + 1) * cols] for k in range(ncl)], 0)
    )
    hs[...] = (dot(high, spread) + dot(low, spread)).reshape(ncl, 8, wide)
    hb[i] = hs[i]

    wait(s1_buf, s1_sems.at[1])
    hear(1)
    tell(2)
    across = [modes8[:, 0:TOP]]
    for f in range(4):
        block = jnp.concatenate([s1_buf[f, 0:8, :], jnp.zeros((8, TOP - 128), F32)], 1)
        across.append(-pltpu.roll(block, first[f], 1))
    pack(0, TOP, jnp.concatenate(across, 0))

    def times(parts, field):
        high, low = split(field)
        both = dot(parts[...], high)
        return both[0:40] + both[48:88] + dot(parts[0:48, :], low)[0:40]

    def assemble(ref, k):
        wait(f_buf.at[k], f_sems.at[k, 1])
        for f in range(4):
            pad[f, TOP : TOP + CAP, :] = f_buf[k, f]
        top = ref[0:TOP, :]
        for f in range(4):
            top = top - pad[f, pl.ds(TOP - first[f], TOP), :]
        ref[0:TOP, :] = top

    def send_faces(ref, k):
        for f in range(4):
            f_send[k, f] = face_of(ref, f)
            send(f_send.at[k, f], f_buf.at[k, f ^ 1], f_sems.at[k], at_step(f + 1))

    def send_terms(terms, k):
        q_send[k] = terms[8:40].reshape(4, 8, 128)
        for f in range(4):
            send(q_send.at[k, f], q_buf.at[k, f ^ 1], q_sems.at[k], at_step(f + 1))
        return terms[0:8]

    def received_terms(k):
        wait(q_buf.at[k], q_sems.at[k, 1])
        return q_buf[k, 0] + q_buf[k, 1] + q_buf[k, 2] + q_buf[k, 3]

    def inner_rows(product):
        return jnp.sum(product, 0, keepdims=True)

    def weighted(field):
        top_rows = lax.broadcasted_iota(jnp.int32, (TOP, 128), 0)
        square = field * field
        return inner_rows(square) - 0.5 * inner_rows(
            jnp.where(top_rows < in_faces, square[0:TOP], 0.0)
        )

    def gather(buf, sems, k, tile):
        mine = buf.at[k, j, pl.ds(0, 6)]
        buf[k, j] = tile
        over_members(lambda peer: send(mine, mine, sems.at[k], (i, peer)))

    def gathered(buf, sems, k):
        wait(buf.at[k, 0 : nme - 1, pl.ds(0, 6)], sems.at[k, 1])
        return split(buf[k].reshape(wide, 128))

    def two_part(matrix, parts):
        high, low = parts
        return dot(matrix[...], jnp.concatenate([high, high], 0)) + dot(matrix[:, 0:wide], low)

    def scatter(k):
        if k == 0:
            part = two_part(h2, gathered(g_buf, g_sems, 0))
        else:
            base = two_part(h2, gathered(e_buf, e_sems, k - 1))
            part = base - two_part(m2, gathered(g_buf, g_sems, k))
        t_send[k] = part.reshape(ncl, 8, 128)
        t_buf[k, i] = t_send[k, i]
        over_cluster(
            lambda peer: send(
                t_send.at[k, peer, pl.ds(0, 6)], t_buf.at[k, i, pl.ds(0, 6)], t_sems.at[k], (peer, j)
            )
        )

    def share(k):
        wait(t_buf.at[k, 0 : ncl - 1, pl.ds(0, 6)], t_sems.at[k, 1])
        tile = jnp.where(tile_row < 6, jnp.sum(t_buf[k], 0), 0.0)
        c_buf[k, 0] = tile
        mine = c_buf.at[k, 0, pl.ds(0, 6)]
        for slot in range(1, 5):
            send(mine, c_buf.at[k, opposite(slot), pl.ds(0, 6)], c_sems.at[k], at_step(slot))
        if k < 2:
            gather(g_buf, g_sems, k + 1, tile)

    def alone(k):
        return jnp.concatenate([c_buf[k, 0], jnp.zeros((32, 128), F32)], 0)

    def near(k):
        wait(c_buf.at[k, 1:5, pl.ds(0, 6)], c_sems.at[k, 1])
        return c_buf[k].reshape(40, 128)

    def apply(out, field, columns):
        both = dot(ops[:, columns], jnp.concatenate(split(field[columns, :]), 1))
        return out + both[:, 0:128] + both[:, 128:256]

    upper, lower = slice(0, TOP), slice(TOP, slots)

    starts = jnp.concatenate([start8] + [s1_buf[f, 8:16, :] for f in range(4)], 0)
    m_ref[0:TOP, :] = expand(starts, 0, TOP)
    r_ref[...] = r_ref[...] - dot(ops[:, 0:TOP], m_ref[0:TOP, :].astype(BF16))
    own = send_terms(times(bt, r_ref[...]), 0)

    hear(2)
    over_cluster(lambda peer: send(hs.at[peer], hb.at[i], h_sems, (peer, j)))
    gather(g_buf, g_sems, 0, own + received_terms(0))
    send_faces(r_ref, 0)

    both = dot(bt[...], ops[...])
    high, low = split(both[0:48] + both[48:96])
    ft[0:48, :] = high
    ft[48:96, :] = low
    both = dot(ft[...], bb[...])
    x = both[0:40] + both[48:88] + pltpu.roll(both[0:40], 48, 1)
    x = jnp.where(lax.broadcasted_iota(jnp.int32, (40, 128), 1) < 40, x, 0.0)
    mine = x_buf.at[j]
    x_buf[j] = (
        x[0:16]
        + pltpu.roll(x[16:32], 40, 1)
        + pltpu.roll(jnp.concatenate([x[32:40], jnp.zeros((8, 128), F32)], 0), 80, 1)
    )
    over_members(lambda peer: send(mine, mine, x_sems, (i, peer)))

    wait(hb.at[0 : ncl - 1], h_sems.at[1])
    high, low = split(hb[...].reshape(8 * ncl, wide))
    h2[:, 0:wide] = high
    h2[:, wide : 2 * wide] = low
    assemble(r_ref, 0)
    gr_own = send_terms(times(ft, r_ref[...]), 1)
    scatter(0)
    for n, step in enumerate((2, 1)):
        send(hb.at[:, pl.ds(0, 6)], h_near.at[n, :, pl.ds(0, 6)], near_sems.at[n], at_step(step))
    gather(e_buf, e_sems, 0, gr_own + received_terms(1))

    wait(x_buf.at[0 : nme - 1], x_sems.at[1])
    lanes = 5 * wide
    q_row = lax.broadcasted_iota(jnp.int32, (128, lanes), 0)
    q_lane = lax.broadcasted_iota(jnp.int32, (128, lanes), 1)
    source = (q_lane // wide) * 8 + q_lane % 8
    for n in range(5):
        q = (q_row == source + 40 * (n // 2)).astype(BF16)
        half = 8 * (n % 2)
        high, low = split(x_buf[:, half : half + 8, :].reshape(wide, 128))
        d_row = lax.broadcasted_iota(jnp.int32, (wide, lanes), 0)
        d_lane = lax.broadcasted_iota(jnp.int32, (wide, lanes), 1)
        same = d_row // 8 == (d_lane % wide) // 8
        d_high[n * wide : (n + 1) * wide, :] = jnp.where(same, dot(high, q), 0.0).astype(BF16)
        d_low[n * wide : (n + 1) * wide, :] = jnp.where(same, dot(low, q), 0.0).astype(BF16)
    share(0)
    for n in range(2):
        wait(h_near.at[n, :, pl.ds(0, 6)], near_sems.at[n, 1])
    mid = hb[...].reshape(8 * ncl, wide)
    groups = [mid] + [h_near[n].reshape(8 * ncl, wide) for n in range(2)]
    groups += [pltpu.roll(mid, 8, 1), pltpu.roll(mid, wide - 8, 1)]
    for n, group in enumerate(groups):
        high, low = split(group)
        a_high[:, n * wide : (n + 1) * wide] = high
        a_low[:, n * wide : (n + 1) * wide] = low

    def group_of(n):
        at = slice(n * wide, (n + 1) * wide)
        return (
            dot(a_high[...], d_high[:, at]) + dot(a_high[...], d_low[:, at]) + dot(a_low[...], d_high[:, at])
        )

    for n in range(2):
        v_send[n] = group_of(n + 1).reshape(ncl, 8, wide)
        send(
            v_send.at[n, :, pl.ds(0, 6)], v_buf.at[n, :, pl.ds(0, 6)], v_sems.at[n], at_step(n + 1)
        )
    v_ref[0 : 8 * ncl, 0:wide] = (
        group_of(0) + pltpu.roll(group_of(3), wide - 8, 1) + pltpu.roll(group_of(4), 8, 1)
    )

    p0_ref[lower, :] = r_ref[lower, :] - expand(alone(0), TOP)
    u0_ref[...] = apply(0.0, p0_ref, lower)
    p0_ref[upper, :] = r_ref[upper, :] - expand(near(0), 0, TOP)
    u0_ref[...] = apply(u0_ref[...], p0_ref, upper)
    send_faces(u0_ref, 1)
    for n in range(2):
        wait(v_buf.at[n, :, pl.ds(0, 6)], v_sems.at[n, 1])
    high, low = split(
        v_ref[0 : 8 * ncl, 0:wide]
        + v_buf[0].reshape(8 * ncl, wide)
        + v_buf[1].reshape(8 * ncl, wide)
    )
    m2[:, 0:wide] = high
    m2[:, wide : 2 * wide] = low
    scatter(1)
    im_ref[...] = u0_ref[...]
    assemble(im_ref, 1)
    gi_own = send_terms(times(ft, im_ref[...]), 2)
    sum_rows = [weighted(p0_ref[...]), inner_rows(p0_ref[...] * u0_ref[...])]
    gather(e_buf, e_sems, 1, gi_own + received_terms(2))
    share(1)

    q_ref[lower, :] = im_ref[lower, :] - expand(alone(1), TOP)
    v_ref[...] = apply(0.0, q_ref, lower)
    q_ref[upper, :] = im_ref[upper, :] - expand(near(1), 0, TOP)
    v_ref[...] = apply(v_ref[...], q_ref, upper)
    sum_rows += [
        weighted(q_ref[...]),
        inner_rows(q_ref[...] * v_ref[...]),
        inner_rows(p0_ref[...] * v_ref[...] + q_ref[...] * u0_ref[...]),
    ]
    in_face = lax.broadcasted_iota(jnp.int32, (TOP, 128), 0) < in_faces
    cross = p0_ref[...] * q_ref[...]
    sum_rows.append(inner_rows(cross) - 0.5 * inner_rows(jnp.where(in_face, cross[upper], 0.0)))
    sg_buf[j] = jnp.concatenate(sum_rows, 0)
    mine = sg_buf.at[j]
    over_members(lambda peer: send(mine, mine, sg_sems, (i, peer)))
    send_faces(v_ref, 2)
    scatter(2)
    wait(sg_buf.at[0 : nme - 1], sg_sems.at[1])
    st_send[...] = jnp.sum(sg_buf[...], 0)
    st_buf[i] = st_send[...]
    over_cluster(lambda peer: send(st_send, st_buf.at[i], st_sems, (peer, j)))
    assemble(v_ref, 2)
    share(2)
    v_ref[lower, :] = v_ref[lower, :] - expand(alone(2), TOP)
    wait(st_buf.at[0 : ncl - 1], st_sems.at[1])
    total = jnp.sum(st_buf[...], 0)
    norm0, curv0, norm_q, curv_q, curv_pq, norm_pq = [total[n : n + 1] for n in range(6)]
    alpha0 = norm0 / curv0
    norm1 = norm0 - alpha0 * (2.0 * norm_pq - alpha0 * norm_q)
    beta = norm1 / norm0
    scale = 1.0 + beta
    alpha1 = norm1 / (scale * (scale * curv0 - alpha0 * curv_pq) + alpha0 * alpha0 * curv_q)
    first_by = alpha0 + alpha1 * scale
    second_by = alpha0 * alpha1
    m_ref[...] = m_ref[...] + first_by * p0_ref[...] - second_by * q_ref[...]
    store(0, m_ref, m_hbm, 0, slots).start()
    p_ref[lower, :] = p0_ref[lower, :] - first_by * q_ref[lower, :] + second_by * v_ref[lower, :]
    store(1, p_ref, p_hbm, TOP, slots).start()
    last = p0_ref[upper, :] - first_by * q_ref[upper, :] + second_by * v_ref[upper, :]
    p_ref[upper, :] = last - second_by * expand(near(2), 0, TOP)
    store(2, p_ref, p_hbm, 0, TOP).start()

    store(0, m_ref, m_hbm, 0, slots).wait()
    store(1, p_ref, p_hbm, TOP, slots).wait()
    store(2, p_ref, p_hbm, 0, TOP).wait()
    wait(s1_buf, s1_sems.at[0])
    wait(hb.at[0 : ncl - 1], h_sems.at[0])
    wait(x_buf.at[0 : nme - 1], x_sems.at[0])
    for n in range(2):
        wait(h_near.at[n, :, pl.ds(0, 6)], near_sems.at[n, 0])
        wait(v_buf.at[n, :, pl.ds(0, 6)], v_sems.at[n, 0])
        wait(e_buf.at[n, 0 : nme - 1, pl.ds(0, 6)], e_sems.at[n, 0])
    for k in range(3):
        wait(q_buf.at[k], q_sems.at[k, 0])
        wait(f_buf.at[k], f_sems.at[k, 0])
        wait(g_buf.at[k, 0 : nme - 1, pl.ds(0, 6)], g_sems.at[k, 0])
        wait(t_buf.at[k, 0 : ncl - 1, pl.ds(0, 6)], t_sems.at[k, 0])
        wait(c_buf.at[k, 1:5, pl.ds(0, 6)], c_sems.at[k, 0])
    wait(sg_buf.at[0 : nme - 1], sg_sems.at[0])
    wait(st_buf.at[0 : ncl - 1], st_sems.at[0])


UNROLL = True
PIECES = 4


def finish(m_in, p_in, m_out, p_out, held, sems):
    size = m_in.shape[0] // PIECES
    pairs = [
        (src.at[pl.ds(n * size, size)], held.at[k, n], dst.at[pl.ds(n * size, size)], sems.at[0, k, n], sems.at[1, k, n])
        for k, (src, dst) in enumerate(((m_in, m_out), (p_in, p_out)))
        for n in range(PIECES)
    ]
    for src, here, _, sem, _ in pairs:
        pltpu.make_async_copy(src, here, sem).start()
    for src, here, dst, sem, sem2 in pairs:
        pltpu.make_async_copy(src, here, sem).wait()
        pltpu.make_async_copy(here, dst, sem2).start()
    for _, here, dst, _, sem2 in pairs:
        pltpu.make_async_copy(here, dst, sem2).wait()


def solution(mesh):
    ncl, nme = mesh.shape["cluster"], mesh.shape["member"]
    nx = 4 if ncl % 4 == 0 else 1

    def per_device(dual_ops, dual_rhs, rigid_modes, coarse_rows, start_coeffs, face_counts):
        slots, cases = dual_rhs.shape[2:]
        field = pltpu.VMEM((slots, cases), F32)
        out = jax.ShapeDtypeStruct((slots, cases), F32)

        def by_row(x):
            return x.reshape(x.shape[2], 1, x.shape[3])

        multipliers, projected = pl.pallas_call(
            functools.partial(kernel, ncl, nme, nx),
            out_shape=(out, out),
            in_specs=[pl.BlockSpec(memory_space=pltpu.HBM)] * 5
            + [pl.BlockSpec(memory_space=pltpu.SMEM)],
            out_specs=(pl.BlockSpec(memory_space=pl.ANY),) * 2,
            scratch_shapes=[
                field, field,
                pltpu.VMEM((slots, slots), BF16),
                field,
                pltpu.VMEM((6, 1, slots), F32),
                pltpu.VMEM((6, 1, 6 * ncl * nme), F32),
                pltpu.VMEM((6, 1, cases), F32),
                pltpu.VMEM((slots, 128), BF16),
                pltpu.VMEM((96, slots), BF16),
                pltpu.VMEM((96, slots), BF16),
                pltpu.VMEM((4, 2 * TOP + CAP, cases), F32),
                pltpu.VMEM((ncl, 8, 8 * nme), F32),
                pltpu.VMEM((ncl, 8, 8 * nme), F32),
                pltpu.VMEM((8 * ncl, 16 * nme), BF16),
                pltpu.VMEM((8 * ncl, 16 * nme), BF16),
                pltpu.VMEM((2, ncl, 8, 8 * nme), F32),
                pltpu.VMEM((8 * ncl, 40 * nme), BF16),
                pltpu.VMEM((8 * ncl, 40 * nme), BF16),
                pltpu.VMEM((40 * nme, 40 * nme), BF16),
                pltpu.VMEM((40 * nme, 40 * nme), BF16),
                pltpu.VMEM((2, ncl, 8, 8 * nme), F32),
                pltpu.VMEM((2, ncl, 8, 8 * nme), F32),
                field, field, field, field, field, field,
                pltpu.VMEM((4, 16, cases), F32),
                pltpu.VMEM((4, 16, cases), F32),
                pltpu.VMEM((3, 4, 8, cases), F32),
                pltpu.VMEM((3, 4, 8, cases), F32),
                pltpu.VMEM((3, 4, CAP, cases), F32),
                pltpu.VMEM((3, 4, CAP, cases), F32),
                pltpu.VMEM((3, nme, 8, cases), F32),
                pltpu.VMEM((2, nme, 8, cases), F32),
                pltpu.VMEM((nme, 16, 128), F32),
                pltpu.VMEM((3, ncl, 8, cases), F32),
                pltpu.VMEM((3, ncl, 8, cases), F32),
                pltpu.VMEM((3, 5, 8, cases), F32),
                pltpu.VMEM((nme, 6, cases), F32),
                pltpu.VMEM((ncl, 6, cases), F32),
                pltpu.VMEM((6, cases), F32),
                pltpu.SemaphoreType.REGULAR((3,)),
                pltpu.SemaphoreType.DMA((8,)),
                pltpu.SemaphoreType.DMA((2,)),
                pltpu.SemaphoreType.DMA((2,)),
                pltpu.SemaphoreType.DMA((3, 2)),
                pltpu.SemaphoreType.DMA((3, 2)),
                pltpu.SemaphoreType.DMA((3, 2)),
                pltpu.SemaphoreType.DMA((2, 2)),
                pltpu.SemaphoreType.DMA((2,)),
                pltpu.SemaphoreType.DMA((2, 2)),
                pltpu.SemaphoreType.DMA((2, 2)),
                pltpu.SemaphoreType.DMA((3, 2)),
                pltpu.SemaphoreType.DMA((3, 2)),
                pltpu.SemaphoreType.DMA((2,)),
                pltpu.SemaphoreType.DMA((2,)),
            ],
            compiler_params=pltpu.CompilerParams(
                collective_id=0, has_side_effects=True, vmem_limit_bytes=60 << 20
            ),
            name="cg",
        )(
            dual_ops[0, 0], dual_rhs[0, 0], by_row(rigid_modes), by_row(coarse_rows),
            by_row(start_coeffs), face_counts[0, 0],
        )
        multipliers, projected = pl.pallas_call(
            finish,
            out_shape=(out, out),
            in_specs=[pl.BlockSpec(memory_space=pl.ANY)] * 2,
            out_specs=(pl.BlockSpec(memory_space=pl.ANY),) * 2,
            scratch_shapes=[pltpu.VMEM((2, PIECES, slots // PIECES, cases), F32), pltpu.SemaphoreType.DMA((2, 2, PIECES))],
            name="finish",
        )(multipliers, projected)
        return multipliers[None, None], projected[None, None]

    whole = P("cluster", "member", None, None)
    return jax.shard_map(
        per_device,
        mesh=mesh,
        in_specs=(whole,) * 5 + (P("cluster", "member", None),),
        out_specs=(whole, whole),
        check_vma=False,
    )
```

```python
import functools

import jax
import jax.numpy as jnp
from jax import lax
from jax.experimental import pallas as pl
from jax.experimental.pallas import tpu as pltpu
from jax.sharding import PartitionSpec as P

CAP = 64
TOP = 4 * CAP
MESH = pl.DeviceIdType.MESH
F32 = jnp.float32
BF16 = jnp.bfloat16

STEPS = (
    (0, 0), (-1, 0), (1, 0), (0, -1), (0, 1),
)


def opposite(slot):
    return STEPS.index((-STEPS[slot][0], -STEPS[slot][1]))


def dot(a, b):
    return jnp.dot(a, b, preferred_element_type=F32)


def split(x):
    high = x.astype(BF16)
    return high, (x - high.astype(F32)).astype(BF16)


def far_first(t, n):
    return n // 2 + ((t % 2) * 2 - 1) * ((t + 1) // 2)


def kernel(
    ncl, nme, nx,
    ops_hbm, rhs_hbm, modes_hbm, rows_hbm, start_hbm, counts,
    m_hbm, p_hbm,
    m_ref, p_ref, ops, rhs, modes, rows, start,
    bb, bt, ft, pad, hs, hb, h2, m2, h_near, a_high, a_low, d_high, d_low, v_send, v_buf,
    v_ref, r_ref, p0_ref, u0_ref, q_ref, im_ref,
    s1_send, s1_buf, q_send, q_buf, f_send, f_buf,
    g_buf, e_buf, x_buf, t_buf, t_send, c_buf, sg_buf, st_buf, st_send,
    news, local_sem, s1_sems, h_sems, q_sems, f_sems, g_sems, e_sems, x_sems, near_sems, v_sems,
    t_sems, c_sems, sg_sems, st_sems,
):
    i, j = lax.axis_index("cluster"), lax.axis_index("member")
    nz = ncl // nx
    wide, cols = 8 * nme, 6 * nme
    slots = ops.shape[0]

    def at_step(slot):
        di, dj = STEPS[slot]
        return lax.rem(i + (di + ncl), ncl), lax.rem(j + (dj + nme), nme)

    def member_peer(t):
        return lax.rem(j + far_first(t, nme), nme)

    def cluster_peer(t):
        z = lax.rem(i // nx + far_first(t // nx, nz), nz)
        x = lax.rem(i % nx + far_first(t % nx, nx), nx)
        return z * nx + x

    def over_members(body):
        lax.fori_loop(0, nme - 1, lambda t, _: (body(member_peer(t)), 0)[1], 0, unroll=UNROLL)

    def over_cluster(body):
        lax.fori_loop(0, ncl - 1, lambda t, _: (body(cluster_peer(t)), 0)[1], 0, unroll=UNROLL)

    def send(src, dst, sems, device):
        pltpu.make_async_remote_copy(
            src, dst, sems.at[0], sems.at[1], device_id=device, device_id_type=MESH
        ).start()

    def store(n, src, dst, lo, hi):
        return pltpu.make_async_copy(src.at[lo:hi], dst.at[lo:hi], local_sem.at[5 + n])

    def wait(ref, sem):
        pltpu.make_async_copy(ref, ref, sem).wait()

    loads = [
        pltpu.make_async_copy(src, dst, local_sem.at[n])
        for n, (src, dst) in enumerate(
            ((modes_hbm, modes), (start_hbm, start), (rows_hbm, rows), (ops_hbm, ops), (rhs_hbm, rhs))
        )
    ]
    for load in loads:
        load.start()

    barrier = pltpu.get_barrier_semaphore()

    def greet(device):
        pl.semaphore_signal(barrier, inc=1, device_id=device, device_id_type=MESH)

    ny, z, x, y, core = nme // 2, i // nx, i % nx, j // 2, j % 2
    assert nz <= 8 and ny <= 8 and nx in (1, 4)

    def along(axis, step):
        if axis == "z":
            return lax.rem(z + (step + nz), nz) * nx + x, j
        if axis == "x":
            return z * nx + lax.rem(x + (step + nx), nx), j
        return i, lax.rem(y + (step + ny), ny) * 2 + core

    def both_ways(distance, over):
        sizes = (("z", nz), ("y", ny), ("x", nx))
        return [
            along(axis, step) for axis, n in sizes if n > over for step in (-distance, distance)
        ]

    other_core = (i, y * 2 + 1 - core)
    beside = [at_step(slot) for slot in range(1, 5)] + both_ways(1, 1) + [other_core]
    rounds = (
        both_ways(1, 2),
        [along(axis, step) for axis, n in (("z", nz), ("y", ny)) if n > 4 for step in (-2, 2)],
        ([along("x", step) for step in (-1, 1, 2)] if nx > 1 else []) + [other_core],
    )
    for device in beside:
        greet(device)

    def tell(n):
        for device in rounds[n]:
            pl.semaphore_signal(news.at[n], inc=1, device_id=device, device_id_type=MESH)

    def hear(n):
        if rounds[n]:
            pl.semaphore_wait(news.at[n], len(rounds[n]))

    first = [counts[0] * 0, counts[0], counts[0] + counts[1], counts[0] + counts[1] + counts[2]]
    in_faces = first[3] + counts[3]
    face_rows = lax.broadcasted_iota(jnp.int32, (CAP, 128), 0)
    tile_row = lax.broadcasted_iota(jnp.int32, (8, 128), 0)
    tile_lane = lax.broadcasted_iota(jnp.int32, (8, 128), 1)

    def face_of(ref, f):
        block = ref[pl.ds(first[f], CAP), :]
        return jnp.where(face_rows < counts[f], block, 0.0)

    loads[0].wait()
    loads[1].wait()
    modes8 = jnp.concatenate([modes[:, 0, :], jnp.zeros((2, slots), F32)], 0)
    start8 = jnp.concatenate([start[:, 0, :], jnp.zeros((2, 128), F32)], 0)
    for f in range(4):
        turned = pltpu.roll(modes8[:, 0:TOP], lax.rem(TOP - first[f], TOP), 1)[:, 0:128]
        s1_send[f, 0:8, :] = jnp.where(tile_lane < counts[f], turned, 0.0)
        s1_send[f, 8:16, :] = start8

    pl.semaphore_wait(barrier, len(beside))
    for f in range(4):
        send(s1_send.at[f], s1_buf.at[f ^ 1], s1_sems, at_step(f + 1))
    tell(0)

    pad[...] = jnp.zeros_like(pad)
    g_buf[:, :, 6:8, :] = jnp.zeros((3, nme, 2, 128), F32)
    e_buf[:, :, 6:8, :] = jnp.zeros((2, nme, 2, 128), F32)
    c_buf[:, :, 6:8, :] = jnp.zeros((3, 5, 2, 128), F32)

    def pack(lo, hi, across):
        high, low = split(across)
        high, low = high.astype(F32), low.astype(F32)
        none = jnp.zeros((8, hi - lo), F32)
        bt[0:48, lo:hi] = jnp.concatenate([high, none], 0).astype(BF16)
        bt[48:96, lo:hi] = jnp.concatenate([low, none], 0).astype(BF16)
        bb[lo:hi, :] = jnp.concatenate([high, high, low, none], 0).T.astype(BF16)

    def expand(coeffs, lo=0, hi=None):
        high, low = split(coeffs)
        return dot(bb[lo:hi, :], jnp.concatenate([high, low, high, jnp.zeros((8, 128), BF16)], 0))

    hear(0)
    tell(1)

    pack(TOP, slots, jnp.concatenate([modes8[:, TOP:], jnp.zeros((32, slots - TOP), F32)], 0))
    m_ref[TOP:, :] = expand(jnp.concatenate([start8, jnp.zeros((32, 128), F32)], 0), TOP)
    loads[3].wait()
    loads[4].wait()
    r_ref[...] = rhs[...] - dot(ops[:, TOP:], m_ref[TOP:, :].astype(BF16))

    loads[2].wait()
    spread = (
        lax.broadcasted_iota(jnp.int32, (cols, wide), 1)
        == (lax.broadcasted_iota(jnp.int32, (cols, wide), 0) // 6) * 8
        + lax.broadcasted_iota(jnp.int32, (cols, wide), 0) % 6
    ).astype(BF16)
    row_values = jnp.concatenate([rows[:, 0, :], jnp.zeros((2, cols * ncl), F32)], 0)
    high, low = split(
        jnp.concatenate([row_values[:, k * cols : (k + 1) * cols] for k in range(ncl)], 0)
    )
    hs[...] = (dot(high, spread) + dot(low, spread)).reshape(ncl, 8, wide)
    hb[i] = hs[i]

    wait(s1_buf, s1_sems.at[1])
    hear(1)
    tell(2)
    across = [modes8[:, 0:TOP]]
    for f in range(4):
        block = jnp.concatenate([s1_buf[f, 0:8, :], jnp.zeros((8, TOP - 128), F32)], 1)
        across.append(-pltpu.roll(block, first[f], 1))
    pack(0, TOP, jnp.concatenate(across, 0))

    def times(parts, field):
        high, low = split(field)
        both = dot(parts[...], high)
        return both[0:40] + both[48:88] + dot(parts[0:48, :], low)[0:40]

    def assemble(ref, k):
        wait(f_buf.at[k], f_sems.at[k, 1])
        for f in range(4):
            pad[f, TOP : TOP + CAP, :] = f_buf[k, f]
        top = ref[0:TOP, :]
        for f in range(4):
            top = top - pad[f, pl.ds(TOP - first[f], TOP), :]
        ref[0:TOP, :] = top

    def send_faces(ref, k):
        for f in range(4):
            f_send[k, f] = face_of(ref, f)
            send(f_send.at[k, f], f_buf.at[k, f ^ 1], f_sems.at[k], at_step(f + 1))

    def send_terms(terms, k):
        q_send[k] = terms[8:40].reshape(4, 8, 128)
        for f in range(4):
            send(q_send.at[k, f], q_buf.at[k, f ^ 1], q_sems.at[k], at_step(f + 1))
        return terms[0:8]

    def received_terms(k):
        wait(q_buf.at[k], q_sems.at[k, 1])
        return q_buf[k, 0] + q_buf[k, 1] + q_buf[k, 2] + q_buf[k, 3]

    def inner_rows(product):
        return jnp.sum(product, 0, keepdims=True)

    def weighted(field):
        top_rows = lax.broadcasted_iota(jnp.int32, (TOP, 128), 0)
        square = field * field
        return inner_rows(square) - 0.5 * inner_rows(
            jnp.where(top_rows < in_faces, square[0:TOP], 0.0)
        )

    def gather(buf, sems, k, tile):
        mine = buf.at[k, j, pl.ds(0, 6)]
        buf[k, j] = tile
        over_members(lambda peer: send(mine, mine, sems.at[k], (i, peer)))

    def gathered(buf, sems, k):
        wait(buf.at[k, 0 : nme - 1, pl.ds(0, 6)], sems.at[k, 1])
        return split(buf[k].reshape(wide, 128))

    def two_part(matrix, parts):
        high, low = parts
        return dot(matrix[...], jnp.concatenate([high, high], 0)) + dot(matrix[:, 0:wide], low)

    def scatter(k):
        if k == 0:
            part = two_part(h2, gathered(g_buf, g_sems, 0))
        else:
            base = two_part(h2, gathered(e_buf, e_sems, k - 1))
            part = base - two_part(m2, gathered(g_buf, g_sems, k))
        t_send[k] = part.reshape(ncl, 8, 128)
        t_buf[k, i] = t_send[k, i]
        over_cluster(
            lambda peer: send(
                t_send.at[k, peer, pl.ds(0, 6)], t_buf.at[k, i, pl.ds(0, 6)], t_sems.at[k], (peer, j)
            )
        )

    def share(k):
        wait(t_buf.at[k, 0 : ncl - 1, pl.ds(0, 6)], t_sems.at[k, 1])
        tile = jnp.where(tile_row < 6, jnp.sum(t_buf[k], 0), 0.0)
        c_buf[k, 0] = tile
        mine = c_buf.at[k, 0, pl.ds(0, 6)]
        for slot in range(1, 5):
            send(mine, c_buf.at[k, opposite(slot), pl.ds(0, 6)], c_sems.at[k], at_step(slot))
        if k < 2:
            gather(g_buf, g_sems, k + 1, tile)

    def alone(k):
        return jnp.concatenate([c_buf[k, 0], jnp.zeros((32, 128), F32)], 0)

    def near(k):
        wait(c_buf.at[k, 1:5, pl.ds(0, 6)], c_sems.at[k, 1])
        return c_buf[k].reshape(40, 128)

    def apply(out, field, columns):
        both = dot(ops[:, columns], jnp.concatenate(split(field[columns, :]), 1))
        return out + both[:, 0:128] + both[:, 128:256]

    upper, lower = slice(0, TOP), slice(TOP, slots)

    starts = jnp.concatenate([start8] + [s1_buf[f, 8:16, :] for f in range(4)], 0)
    m_ref[0:TOP, :] = expand(starts, 0, TOP)
    r_ref[...] = r_ref[...] - dot(ops[:, 0:TOP], m_ref[0:TOP, :].astype(BF16))
    own = send_terms(times(bt, r_ref[...]), 0)

    hear(2)
    over_cluster(lambda peer: send(hs.at[peer], hb.at[i], h_sems, (peer, j)))
    gather(g_buf, g_sems, 0, own + received_terms(0))
    send_faces(r_ref, 0)

    both = dot(bt[...], ops[...])
    high, low = split(both[0:48] + both[48:96])
    ft[0:48, :] = high
    ft[48:96, :] = low
    both = dot(ft[...], bb[...])
    x = both[0:40] + both[48:88] + pltpu.roll(both[0:40], 48, 1)
    x = jnp.where(lax.broadcasted_iota(jnp.int32, (40, 128), 1) < 40, x, 0.0)
    mine = x_buf.at[j]
    x_buf[j] = (
        x[0:16]
        + pltpu.roll(x[16:32], 40, 1)
        + pltpu.roll(jnp.concatenate([x[32:40], jnp.zeros((8, 128), F32)], 0), 80, 1)
    )
    over_members(lambda peer: send(mine, mine, x_sems, (i, peer)))

    wait(hb.at[0 : ncl - 1], h_sems.at[1])
    high, low = split(hb[...].reshape(8 * ncl, wide))
    h2[:, 0:wide] = high
    h2[:, wide : 2 * wide] = low
    scatter(0)
    assemble(r_ref, 0)
    gr_own = send_terms(times(ft, r_ref[...]), 1)
    for n, step in enumerate((2, 1)):
        send(hb.at[:, pl.ds(0, 6)], h_near.at[n, :, pl.ds(0, 6)], near_sems.at[n], at_step(step))
    gather(e_buf, e_sems, 0, gr_own + received_terms(1))

    wait(x_buf.at[0 : nme - 1], x_sems.at[1])
    lanes = 5 * wide
    q_row = lax.broadcasted_iota(jnp.int32, (128, lanes), 0)
    q_lane = lax.broadcasted_iota(jnp.int32, (128, lanes), 1)
    source = (q_lane // wide) * 8 + q_lane % 8
    for n in range(5):
        q = (q_row == source + 40 * (n // 2)).astype(BF16)
        half = 8 * (n % 2)
        high, low = split(x_buf[:, half : half + 8, :].reshape(wide, 128))
        d_row = lax.broadcasted_iota(jnp.int32, (wide, lanes), 0)
        d_lane = lax.broadcasted_iota(jnp.int32, (wide, lanes), 1)
        same = d_row // 8 == (d_lane % wide) // 8
        d_high[n * wide : (n + 1) * wide, :] = jnp.where(same, dot(high, q), 0.0).astype(BF16)
        d_low[n * wide : (n + 1) * wide, :] = jnp.where(same, dot(low, q), 0.0).astype(BF16)
    share(0)
    for n in range(2):
        wait(h_near.at[n, :, pl.ds(0, 6)], near_sems.at[n, 1])
    mid = hb[...].reshape(8 * ncl, wide)
    groups = [mid] + [h_near[n].reshape(8 * ncl, wide) for n in range(2)]
    groups += [pltpu.roll(mid, 8, 1), pltpu.roll(mid, wide - 8, 1)]
    for n, group in enumerate(groups):
        high, low = split(group)
        a_high[:, n * wide : (n + 1) * wide] = high
        a_low[:, n * wide : (n + 1) * wide] = low

    def group_of(n):
        at = slice(n * wide, (n + 1) * wide)
        return (
            dot(a_high[...], d_high[:, at]) + dot(a_high[...], d_low[:, at]) + dot(a_low[...], d_high[:, at])
        )

    for n in range(2):
        v_send[n] = group_of(n + 1).reshape(ncl, 8, wide)
        send(
            v_send.at[n, :, pl.ds(0, 6)], v_buf.at[n, :, pl.ds(0, 6)], v_sems.at[n], at_step(n + 1)
        )
    v_ref[0 : 8 * ncl, 0:wide] = (
        group_of(0) + pltpu.roll(group_of(3), wide - 8, 1) + pltpu.roll(group_of(4), 8, 1)
    )

    p0_ref[lower, :] = r_ref[lower, :] - expand(alone(0), TOP)
    u0_ref[...] = apply(0.0, p0_ref, lower)
    p0_ref[upper, :] = r_ref[upper, :] - expand(near(0), 0, TOP)
    u0_ref[...] = apply(u0_ref[...], p0_ref, upper)
    send_faces(u0_ref, 1)
    for n in range(2):
        wait(v_buf.at[n, :, pl.ds(0, 6)], v_sems.at[n, 1])
    high, low = split(
        v_ref[0 : 8 * ncl, 0:wide]
        + v_buf[0].reshape(8 * ncl, wide)
        + v_buf[1].reshape(8 * ncl, wide)
    )
    m2[:, 0:wide] = high
    m2[:, wide : 2 * wide] = low
    scatter(1)
    im_ref[...] = u0_ref[...]
    assemble(im_ref, 1)
    gi_own = send_terms(times(ft, im_ref[...]), 2)
    sum_rows = [weighted(p0_ref[...]), inner_rows(p0_ref[...] * u0_ref[...])]
    share(1)
    gather(e_buf, e_sems, 1, gi_own + received_terms(2))

    q_ref[lower, :] = im_ref[lower, :] - expand(alone(1), TOP)
    v_ref[...] = apply(0.0, q_ref, lower)
    q_ref[upper, :] = im_ref[upper, :] - expand(near(1), 0, TOP)
    v_ref[...] = apply(v_ref[...], q_ref, upper)
    sum_rows += [
        weighted(q_ref[...]),
        inner_rows(q_ref[...] * v_ref[...]),
        inner_rows(p0_ref[...] * v_ref[...] + q_ref[...] * u0_ref[...]),
    ]
    in_face = lax.broadcasted_iota(jnp.int32, (TOP, 128), 0) < in_faces
    cross = p0_ref[...] * q_ref[...]
    sum_rows.append(inner_rows(cross) - 0.5 * inner_rows(jnp.where(in_face, cross[upper], 0.0)))
    sg_buf[j] = jnp.concatenate(sum_rows, 0)
    mine = sg_buf.at[j]
    over_members(lambda peer: send(mine, mine, sg_sems, (i, peer)))
    send_faces(v_ref, 2)
    scatter(2)
    wait(sg_buf.at[0 : nme - 1], sg_sems.at[1])
    st_send[...] = jnp.sum(sg_buf[...], 0)
    st_buf[i] = st_send[...]
    over_cluster(lambda peer: send(st_send, st_buf.at[i], st_sems, (peer, j)))
    assemble(v_ref, 2)
    share(2)
    v_ref[lower, :] = v_ref[lower, :] - expand(alone(2), TOP)
    wait(st_buf.at[0 : ncl - 1], st_sems.at[1])
    total = jnp.sum(st_buf[...], 0)
    norm0, curv0, norm_q, curv_q, curv_pq, norm_pq = [total[n : n + 1] for n in range(6)]
    alpha0 = norm0 / curv0
    norm1 = norm0 - alpha0 * (2.0 * norm_pq - alpha0 * norm_q)
    beta = norm1 / norm0
    scale = 1.0 + beta
    alpha1 = norm1 / (scale * (scale * curv0 - alpha0 * curv_pq) + alpha0 * alpha0 * curv_q)
    first_by = alpha0 + alpha1 * scale
    second_by = alpha0 * alpha1
    m_ref[...] = m_ref[...] + first_by * p0_ref[...] - second_by * q_ref[...]
    store(0, m_ref, m_hbm, 0, slots).start()
    p_ref[lower, :] = p0_ref[lower, :] - first_by * q_ref[lower, :] + second_by * v_ref[lower, :]
    store(1, p_ref, p_hbm, TOP, slots).start()
    last = p0_ref[upper, :] - first_by * q_ref[upper, :] + second_by * v_ref[upper, :]
    p_ref[upper, :] = last - second_by * expand(near(2), 0, TOP)
    store(2, p_ref, p_hbm, 0, TOP).start()

    store(0, m_ref, m_hbm, 0, slots).wait()
    store(1, p_ref, p_hbm, TOP, slots).wait()
    store(2, p_ref, p_hbm, 0, TOP).wait()
    wait(s1_buf, s1_sems.at[0])
    wait(hb.at[0 : ncl - 1], h_sems.at[0])
    wait(x_buf.at[0 : nme - 1], x_sems.at[0])
    for n in range(2):
        wait(h_near.at[n, :, pl.ds(0, 6)], near_sems.at[n, 0])
        wait(v_buf.at[n, :, pl.ds(0, 6)], v_sems.at[n, 0])
        wait(e_buf.at[n, 0 : nme - 1, pl.ds(0, 6)], e_sems.at[n, 0])
    for k in range(3):
        wait(q_buf.at[k], q_sems.at[k, 0])
        wait(f_buf.at[k], f_sems.at[k, 0])
        wait(g_buf.at[k, 0 : nme - 1, pl.ds(0, 6)], g_sems.at[k, 0])
        wait(t_buf.at[k, 0 : ncl - 1, pl.ds(0, 6)], t_sems.at[k, 0])
        wait(c_buf.at[k, 1:5, pl.ds(0, 6)], c_sems.at[k, 0])
    wait(sg_buf.at[0 : nme - 1], sg_sems.at[0])
    wait(st_buf.at[0 : ncl - 1], st_sems.at[0])


UNROLL = True
PIECES = 4


def finish(m_in, p_in, m_out, p_out, held, sems):
    size = m_in.shape[0] // PIECES
    pairs = [
        (src.at[pl.ds(n * size, size)], held.at[k, n], dst.at[pl.ds(n * size, size)], sems.at[0, k, n], sems.at[1, k, n])
        for k, (src, dst) in enumerate(((m_in, m_out), (p_in, p_out)))
        for n in range(PIECES)
    ]
    for src, here, _, sem, _ in pairs:
        pltpu.make_async_copy(src, here, sem).start()
    for src, here, dst, sem, sem2 in pairs:
        pltpu.make_async_copy(src, here, sem).wait()
        pltpu.make_async_copy(here, dst, sem2).start()
    for _, here, dst, _, sem2 in pairs:
        pltpu.make_async_copy(here, dst, sem2).wait()


def solution(mesh):
    ncl, nme = mesh.shape["cluster"], mesh.shape["member"]
    nx = 4 if ncl % 4 == 0 else 1

    def per_device(dual_ops, dual_rhs, rigid_modes, coarse_rows, start_coeffs, face_counts):
        slots, cases = dual_rhs.shape[2:]
        field = pltpu.VMEM((slots, cases), F32)
        out = jax.ShapeDtypeStruct((slots, cases), F32)

        def by_row(x):
            return x.reshape(x.shape[2], 1, x.shape[3])

        multipliers, projected = pl.pallas_call(
            functools.partial(kernel, ncl, nme, nx),
            out_shape=(out, out),
            in_specs=[pl.BlockSpec(memory_space=pltpu.HBM)] * 5
            + [pl.BlockSpec(memory_space=pltpu.SMEM)],
            out_specs=(pl.BlockSpec(memory_space=pl.ANY),) * 2,
            scratch_shapes=[
                field, field,
                pltpu.VMEM((slots, slots), BF16),
                field,
                pltpu.VMEM((6, 1, slots), F32),
                pltpu.VMEM((6, 1, 6 * ncl * nme), F32),
                pltpu.VMEM((6, 1, cases), F32),
                pltpu.VMEM((slots, 128), BF16),
                pltpu.VMEM((96, slots), BF16),
                pltpu.VMEM((96, slots), BF16),
                pltpu.VMEM((4, 2 * TOP + CAP, cases), F32),
                pltpu.VMEM((ncl, 8, 8 * nme), F32),
                pltpu.VMEM((ncl, 8, 8 * nme), F32),
                pltpu.VMEM((8 * ncl, 16 * nme), BF16),
                pltpu.VMEM((8 * ncl, 16 * nme), BF16),
                pltpu.VMEM((2, ncl, 8, 8 * nme), F32),
                pltpu.VMEM((8 * ncl, 40 * nme), BF16),
                pltpu.VMEM((8 * ncl, 40 * nme), BF16),
                pltpu.VMEM((40 * nme, 40 * nme), BF16),
                pltpu.VMEM((40 * nme, 40 * nme), BF16),
                pltpu.VMEM((2, ncl, 8, 8 * nme), F32),
                pltpu.VMEM((2, ncl, 8, 8 * nme), F32),
                field, field, field, field, field, field,
                pltpu.VMEM((4, 16, cases), F32),
                pltpu.VMEM((4, 16, cases), F32),
                pltpu.VMEM((3, 4, 8, cases), F32),
                pltpu.VMEM((3, 4, 8, cases), F32),
                pltpu.VMEM((3, 4, CAP, cases), F32),
                pltpu.VMEM((3, 4, CAP, cases), F32),
                pltpu.VMEM((3, nme, 8, cases), F32),
                pltpu.VMEM((2, nme, 8, cases), F32),
                pltpu.VMEM((nme, 16, 128), F32),
                pltpu.VMEM((3, ncl, 8, cases), F32),
                pltpu.VMEM((3, ncl, 8, cases), F32),
                pltpu.VMEM((3, 5, 8, cases), F32),
                pltpu.VMEM((nme, 6, cases), F32),
                pltpu.VMEM((ncl, 6, cases), F32),
                pltpu.VMEM((6, cases), F32),
                pltpu.SemaphoreType.REGULAR((3,)),
                pltpu.SemaphoreType.DMA((8,)),
                pltpu.SemaphoreType.DMA((2,)),
                pltpu.SemaphoreType.DMA((2,)),
                pltpu.SemaphoreType.DMA((3, 2)),
                pltpu.SemaphoreType.DMA((3, 2)),
                pltpu.SemaphoreType.DMA((3, 2)),
                pltpu.SemaphoreType.DMA((2, 2)),
                pltpu.SemaphoreType.DMA((2,)),
                pltpu.SemaphoreType.DMA((2, 2)),
                pltpu.SemaphoreType.DMA((2, 2)),
                pltpu.SemaphoreType.DMA((3, 2)),
                pltpu.SemaphoreType.DMA((3, 2)),
                pltpu.SemaphoreType.DMA((2,)),
                pltpu.SemaphoreType.DMA((2,)),
            ],
            compiler_params=pltpu.CompilerParams(
                collective_id=0, has_side_effects=True, vmem_limit_bytes=60 << 20
            ),
            name="cg",
        )(
            dual_ops[0, 0], dual_rhs[0, 0], by_row(rigid_modes), by_row(coarse_rows),
            by_row(start_coeffs), face_counts[0, 0],
        )
        multipliers, projected = pl.pallas_call(
            finish,
            out_shape=(out, out),
            in_specs=[pl.BlockSpec(memory_space=pl.ANY)] * 2,
            out_specs=(pl.BlockSpec(memory_space=pl.ANY),) * 2,
            scratch_shapes=[pltpu.VMEM((2, PIECES, slots // PIECES, cases), F32), pltpu.SemaphoreType.DMA((2, 2, PIECES))],
            name="finish",
        )(multipliers, projected)
        return multipliers[None, None], projected[None, None]

    whole = P("cluster", "member", None, None)
    return jax.shard_map(
        per_device,
        mesh=mesh,
        in_specs=(whole,) * 5 + (P("cluster", "member", None),),
        out_specs=(whole, whole),
        check_vma=False,
    )
```
